512 devices in a mesh: ctx: 64 (over x, y, core), head: 8 (over z).
Axes of the slice: x: 4, y: 8, z: 8, core: 2. Of those that a mesh axis runs over, the one named last changes fastest.
Arguments:
- queries: bfloat16 [32768, 4096], P(('ctx', 'head')), may hold values from -48 to 48
- keys: bfloat16 [32768, 4096], P(('ctx', 'head')), may hold values from -6 to 6
- values: bfloat16 [32768, 4096], P(('ctx', 'head')), may hold values from -6 to 6
- rates: float32 [32768, 8], P('ctx', 'head'), may hold values from 0.00016572815 to 0.0016572815
- fast_gate: float32 [8, 512, 512], P('head'), may hold values from -0.25 to 0.25
- fast_up: float32 [8, 512, 512], P('head'), may hold values from -0.25 to 0.25
- fast_down: float32 [8, 512, 512], P('head'), may hold values from -0.25 to 0.25
- out_gain: float32 [4096], P('head'), may hold values from 0.5 to 1.5
Outputs:
- mixed: bfloat16 [32768, 4096], P('ctx', 'head')
The draws below stay inside these ranges and needn't reach their ends.
All inputs are finite; a program needn't handle non-finite values.
Results may differ from the reference program's by a relative error of at most 0.012.
Values may be sent and summed in bfloat16 or wider, within the bound.
A program may use at most 64 MiB of HBM per device.

```python
import math
import jax
import jax.numpy as jnp
from jax import lax

D = 4096
AHEADS = 32
FHEADS = 8
WINDOW = 1024
AHD = 128
FD = 512
TOKENS = 32768


def drawn_pair(key):
    base = jax.random.fold_in(key, 7)
    key_query, key_key = jax.random.split(base, 2)
    query_draw = jnp.clip(2.0 * jax.random.normal(key_query, (TOKENS, D), jnp.float32), -12.0, 12.0)
    key_draw = jnp.clip(jax.random.normal(key_key, (TOKENS, D), jnp.float32), -6.0, 6.0)
    return (query_draw, key_draw)


def draw_queries(key, part):
    return drawn_pair(key)[0].astype(jnp.bfloat16)


def draw_keys(key, part):
    return drawn_pair(key)[1].astype(jnp.bfloat16)


def block_scale(stream_key, shape, cuts, least, largest):
    def one(axis_at, parts):
        heights = jax.random.uniform(jax.random.fold_in(jax.random.fold_in(stream_key, 6), axis_at), (parts,), jnp.float32, least / len(cuts), largest / len(cuts))
        return jnp.repeat(jnp.exp(heights), shape[axis_at] // parts).reshape((-1,) + (1,) * (len(shape) - axis_at - 1))

    gain = one(*cuts[0])
    for cut in cuts[1:]:
        gain = gain * one(*cut)
    return gain


def noise(key, extent, deviation, reach, pieces=(), kind=jnp.bfloat16):
    values = deviation * jax.random.normal(key, extent, jnp.float32)
    if pieces:
        values = values * block_scale(key, extent, pieces, -0.22, 0.18)
    return jnp.clip(values, -reach, reach).astype(kind)


def setup_inputs(seed: int = 0) -> dict:
    seeds = jax.random.split(jax.random.key(seed), 9)
    queries = draw_queries(jax.random.fold_in(seeds[8], 71), 0)
    keys = draw_keys(jax.random.fold_in(seeds[8], 71), 0)
    values = noise(seeds[2], (TOKENS, D), 1.0, 6.0, ((0, 512),))
    rates = jnp.clip(jnp.exp(math.log(0.0016572815) - 2.3025851 * jax.random.uniform(seeds[3], (TOKENS, FHEADS), jnp.float32) ** block_scale(seeds[3], (TOKENS, FHEADS), ((0, 64), (1, 8)), -0.2, 0.2)), 0.00016572815, 0.0016572815)
    fast_gate = noise(seeds[4], (FHEADS, FD, FD), FD ** -0.5, 0.25, ((0, 8),), jnp.float32)
    fast_up = noise(seeds[5], (FHEADS, FD, FD), FD ** -0.5, 0.25, ((0, 8),), jnp.float32)
    fast_down = noise(seeds[6], (FHEADS, FD, FD), FD ** -0.5, 0.25, ((0, 8),), jnp.float32)
    out_gain = jnp.clip(1.0 + 0.1 * jax.random.normal(seeds[7], (D,), jnp.float32), 0.5, 1.5)
    return dict(queries=queries, keys=keys, values=values, rates=rates, fast_gate=fast_gate, fast_up=fast_up, fast_down=fast_down, out_gain=out_gain)


epsilon = 1e-06
rms_epsilon = 1e-05

def silu_slope(pre):
    sigma = jax.nn.sigmoid(pre)
    return sigma * (1.0 + pre * (1.0 - sigma))

def column_norms(matrix):
    return jnp.sqrt(lax.optimization_barrier(jnp.sum(matrix * matrix, axis=-2)) + epsilon)

def window_attention(queries, keys, values):
    scale = 1.0 / math.sqrt(AHD)
    query_all = queries.astype(jnp.float32).reshape(TOKENS, AHEADS, AHD)
    front = jnp.zeros((WINDOW, AHEADS, AHD), jnp.float32)
    key_all = jnp.concatenate([front, keys.astype(jnp.float32).reshape(TOKENS, AHEADS, AHD)], 0)
    value_all = jnp.concatenate([front, values.astype(jnp.float32).reshape(TOKENS, AHEADS, AHD)], 0)

    def per_block(block):
        start = block * WINDOW
        query_block = lax.dynamic_slice_in_dim(query_all, start, WINDOW, 0)
        key_block = lax.dynamic_slice_in_dim(key_all, start, 2 * WINDOW, 0)
        value_block = lax.dynamic_slice_in_dim(value_all, start, 2 * WINDOW, 0)
        scores = jnp.einsum('qhd,khd->hqk', query_block, key_block) * scale
        query_pos = start + jnp.arange(WINDOW, dtype=jnp.int32)
        key_pos = start - WINDOW + jnp.arange(2 * WINDOW, dtype=jnp.int32)
        allowed = (key_pos[None, :] <= query_pos[:, None]) & (key_pos[None, :] > query_pos[:, None] - WINDOW) & (key_pos[None, :] >= 0)
        scores = jnp.where(allowed[None], scores, -1e+30)
        peak = lax.optimization_barrier(jnp.max(scores, axis=-1, keepdims=True))
        expo = jnp.exp(scores - peak)
        weights = (expo / lax.optimization_barrier(jnp.sum(expo, axis=-1, keepdims=True))).astype(jnp.bfloat16)
        return jnp.einsum('hqk,khd->qhd', weights.astype(jnp.float32), value_block)
    blocks = lax.map(per_block, jnp.arange(TOKENS // WINDOW, dtype=jnp.int32))
    return blocks.reshape(TOKENS, D)

def fast_head(inputs):
    query_rows, key_rows, value_rows, rate_col, gate_init, up_init, down_init, gain_row = inputs
    gate_cast = gate_init.astype(jnp.bfloat16)
    up_cast = up_init.astype(jnp.bfloat16)
    down_cast = down_init.astype(jnp.bfloat16)
    pre_gate = jnp.dot(key_rows, gate_cast, preferred_element_type=jnp.float32)
    pre_up = jnp.dot(key_rows, up_cast, preferred_element_type=jnp.float32)
    hidden = (jax.nn.silu(pre_gate) * pre_up).astype(jnp.bfloat16)
    target = (rate_col[:, None] * value_rows.astype(jnp.float32)).astype(jnp.bfloat16)
    step_down = jnp.dot(hidden.T, target, preferred_element_type=jnp.float32)
    back = jnp.dot(target, down_cast.T, preferred_element_type=jnp.float32)
    grad_gate = (back * pre_up * silu_slope(pre_gate)).astype(jnp.bfloat16)
    grad_up = (back * jax.nn.silu(pre_gate)).astype(jnp.bfloat16)
    step_gate = jnp.dot(key_rows.T, grad_gate, preferred_element_type=jnp.float32)
    step_up = jnp.dot(key_rows.T, grad_up, preferred_element_type=jnp.float32)
    renormed = []
    for initial, step_value in ((gate_init, step_gate), (up_init, step_up), (down_init, step_down)):
        moved = initial + step_value
        renormed.append((moved * (column_norms(initial) / column_norms(moved))[None, :]).astype(jnp.bfloat16))
    read_gate = jnp.dot(query_rows, renormed[0], preferred_element_type=jnp.float32)
    read_up = jnp.dot(query_rows, renormed[1], preferred_element_type=jnp.float32)
    read_hidden = (jax.nn.silu(read_gate) * read_up).astype(jnp.bfloat16)
    read = jnp.dot(read_hidden, renormed[2], preferred_element_type=jnp.float32)
    scale_back = lax.rsqrt(lax.optimization_barrier(jnp.mean(read * read, axis=-1, keepdims=True)) + rms_epsilon)
    return read * scale_back * gain_row[None, :]

def reference(queries, keys, values, rates, fast_gate, fast_up, fast_down, out_gain):
    attended = window_attention(queries, keys, values)

    def by_head(array):
        return array.reshape(TOKENS, FHEADS, FD).transpose(1, 0, 2)
    readout = lax.map(fast_head, (by_head(queries), by_head(keys), by_head(values), rates.T, fast_gate, fast_up, fast_down, out_gain.reshape(FHEADS, FD)))
    readout = readout.transpose(1, 0, 2).reshape(TOKENS, D)
    return (attended + readout).astype(jnp.bfloat16)
```

```python
import functools
import math

import jax
import jax.numpy as jnp
from jax import lax
from jax.experimental import pallas as pl
from jax.experimental.pallas import tpu as pltpu
from jax.sharding import PartitionSpec as P

AHD = 128
TQ = 128
X = 4
EPS = 1e-06
RMS_EPS = 1e-05
NEG = -1e30
MESH = pl.DeviceIdType.MESH
NT = (((1,), (1,)), ((), ()))
TN = (((0,), (0,)), ((), ()))
NN = (((1,), (0,)), ((), ()))
F32 = jnp.float32
BF16 = jnp.bfloat16


def dot(a, b, dims):
    return lax.dot_general(a, b, dims, preferred_element_type=F32)


def sigmoid(a):
    return 1.0 / (1.0 + jnp.exp(-a))


def kernel(
    sizes,
    q_in, k_in, v_in, rates, gate_in, up_in, down_in, gain,
    out,
    qbuf, kbuf, vbuf, weights, casts, hidden, target, ggate, gup,
    part, core_in, xs, x_one, x_two, y_own, y_in, gathered, renormed, attended,
    z_send, z_recv, own_sem, w_sem, h1_send, h1_recv, h2_send, h2_recv,
    c_send, c_recv, x_send, x_recv, y_send, y_recv, g_send, g_recv, gx_send, gx_recv, gc_send, gc_recv,
):
    Y, Z, T, F, B = sizes
    C = 2 * X * Y
    H = F // 2
    G = X * Y
    HY = Y // 2
    rem = lax.rem
    c = lax.axis_index("ctx")
    z = lax.axis_index("head")
    core = rem(c, 2)
    chip = lax.div(c, 2)
    y = rem(chip, Y)
    x = lax.div(chip, Y)
    other = 1 - core
    mate = (c + 1 - 2 * core, z)
    xp, xm, xo = rem(x + 1, X), rem(x + X - 1, X), rem(x + 2, X)

    def at(xx, yy):
        return ((xx * Y + yy) * 2 + core, z)

    def remote(src, dst, send, recv, device):
        return pltpu.make_async_remote_copy(
            src_ref=src, dst_ref=dst, send_sem=send, recv_sem=recv, device_id=device, device_id_type=MESH
        )

    for m, ref in enumerate((gate_in, up_in, down_in)):
        pltpu.make_async_copy(ref, weights.at[m], w_sem.at[m]).start()
    own = pl.ds(2 * T + z * B, B)
    mine = pl.ds(pl.multiple_of(z * F, F), F)
    own_copies = [
        pltpu.make_async_copy(k_in.at[:, mine], kbuf.at[own, :], own_sem.at[0]),
        pltpu.make_async_copy(v_in.at[:, mine], vbuf.at[own, :], own_sem.at[1]),
        pltpu.make_async_copy(q_in.at[:, mine], qbuf.at[pl.ds(z * B, B), :], own_sem.at[2]),
    ]
    for copy in own_copies:
        copy.start()

    barrier = pltpu.get_barrier_semaphore()
    partners = [(c, rem(z + d, Z)) for d in range(1, Z)]
    partners += [at(xp, y), at(xm, y), mate]
    partners += [at(x, rem(y + d, Y)) for d in range(1, Y)]
    partners += [(rem(c + 2, C), z), (rem(c + C - 2, C), z)]
    for partner in partners:
        pl.semaphore_signal(barrier, inc=1, device_id=partner, device_id_type=MESH)
    pl.semaphore_wait(barrier, len(partners))

    def z_copy(which, d):
        src = (k_in, v_in, q_in)[which]
        dst, base = ((kbuf, 2 * T), (vbuf, 2 * T), (qbuf, 0))[which]
        t = rem(z + d, Z)
        return remote(
            src.at[:, pl.ds(pl.multiple_of(t * F, F), F)],
            dst.at[pl.ds(base + z * B, B), :],
            z_send.at[which, d],
            z_recv.at[which, d],
            (c, t),
        )

    order = []
    for d in range(1, Z // 2):
        order += [d, Z - d]
    order.append(Z // 2)
    for d in order:
        z_copy(0, d).start()
        z_copy(1, d).start()

    @pl.when(c == 0)
    def _():
        zeros = jnp.zeros((T, F), BF16)
        kbuf[pl.ds(T, T), :] = zeros
        vbuf[pl.ds(T, T), :] = zeros

    @pl.when(c < 2)
    def _():
        zeros = jnp.zeros((T, F), BF16)
        kbuf[pl.ds(0, T), :] = zeros
        vbuf[pl.ds(0, T), :] = zeros

    for m, ref in enumerate((gate_in, up_in, down_in)):
        pltpu.make_async_copy(ref, weights.at[m], w_sem.at[m]).wait()
    for m in range(3):
        casts[m] = weights[m].astype(BF16)

    def ahead(which, s, first):
        buf = (kbuf, vbuf)[which]
        return remote(
            buf.at[pl.ds(2 * T + s * B, B), :],
            buf.at[pl.ds(s * B, B), :],
            h2_send.at[which, s],
            h2_recv.at[which, s],
            (rem(c + 2, C), z),
        )

    def across(which, s):
        buf = (kbuf, vbuf)[which]
        return remote(
            buf.at[pl.ds((1 - core) * 2 * T + s * B, B), :],
            buf.at[pl.ds(T + s * B, B), :],
            h1_send.at[which, s],
            h1_recv.at[which, s],
            mate,
        )

    def turn(i):
        return jnp.where(rem(i, 2) == 1, lax.div(i + 1, 2), rem(Z - lax.div(i, 2), Z))

    def update(i, carry):
        d = turn(i)
        s = rem(z + Z - d, Z)

        @pl.when(i == 0)
        def _():
            own_copies[0].wait()
            own_copies[1].wait()

        @pl.when(i > 0)
        def _():
            z_copy(0, d).wait_recv()
            z_copy(1, d).wait_recv()

        @pl.when(c + 2 < C)
        def _():
            ahead(0, s, 0).start()
            ahead(1, s, 0).start()

        @pl.when(core == 0)
        def _():
            across(0, s).start()
            across(1, s).start()

        rows = pl.ds(pl.multiple_of(s * B, B), B)
        here = pl.ds(pl.multiple_of(2 * T + s * B, B), B)
        k = kbuf[here, :]
        aim = (rates[rows, :] * vbuf[here, :].astype(F32)).astype(BF16)
        target[rows, :] = aim
        pre_gate = dot(k, casts[0], NN)
        pre_up = dot(k, casts[1], NN)
        back = dot(aim, casts[2], NT)
        sig = sigmoid(pre_gate)
        sil = pre_gate * sig
        hidden[rows, :] = (sil * pre_up).astype(BF16)
        ggate[rows, :] = (back * pre_up * (sig * (1.0 + pre_gate * (1.0 - sig)))).astype(BF16)
        gup[rows, :] = (back * sil).astype(BF16)
        return carry

    lax.fori_loop(0, Z, update, 0)

    for d in order:
        z_copy(2, d).start()

    here = pl.ds(2 * T, T)

    def packed(step):
        low = step[:, :H].reshape(G, 8, H)
        high = step[:, H:].reshape(G, 8, H)
        return jnp.concatenate([low, high], axis=1).astype(BF16)

    def steps(half, carry):
        cols = pl.ds(pl.multiple_of(half * H, H), H)
        rows = pl.ds(half * G, G)
        part[rows, 0:16, :] = packed(dot(ggate[:, cols], kbuf[here, :], TN))
        part[rows, 16:32, :] = packed(dot(gup[:, cols], kbuf[here, :], TN))
        part[rows, 32:48, :] = packed(dot(target[:, cols], hidden[...], TN))
        return carry

    def core_copy(j, xx):
        return remote(
            part.at[pl.ds(other * G + xx * Y, Y)],
            core_in.at[pl.ds(xx * Y, Y)],
            c_send.at[j],
            c_recv.at[j],
            mate,
        )

    blocks = (xo, xp, xm, x)
    steps(other, 0)
    for j in range(4):
        core_copy(j, blocks[j]).start()
    steps(core, 0)

    def chip_sum(j):
        xx = blocks[j]
        core_copy(j, xx).wait_recv()
        total = part[pl.ds(core * G + xx * Y, Y)].astype(F32) + core_in[pl.ds(xx * Y, Y)].astype(F32)
        return total

    def x_copy(j, xx, lo, dst, to):
        return remote(xs.at[pl.ds(xx * Y + lo, HY)], dst, x_send.at[j], x_recv.at[j], to)

    to_p, to_m = at(xp, y), at(xm, y)
    x_copies = [
        x_copy(0, xo, 0, x_one.at[0], to_p),
        x_copy(1, xo, HY, x_one.at[1], to_m),
        x_copy(2, xp, HY, x_two.at[0, pl.ds(HY, HY)], to_p),
        x_copy(3, xm, 0, x_two.at[1, pl.ds(0, HY)], to_m),
        x_copy(4, xp, 0, x_two.at[0, pl.ds(0, HY)], to_p),
        x_copy(5, xm, HY, x_two.at[1, pl.ds(HY, HY)], to_m),
    ]
    xs[pl.ds(xo * Y, Y)] = chip_sum(0).astype(BF16)
    x_copies[0].start()
    x_copies[1].start()
    sum_p = chip_sum(1)
    xs[pl.ds(xp * Y + HY, HY)] = sum_p[HY:].astype(BF16)
    x_copies[2].start()
    sum_m = chip_sum(2)
    xs[pl.ds(xm * Y, HY)] = sum_m[:HY].astype(BF16)
    x_copies[3].start()
    x_copies[0].wait_recv()
    xs[pl.ds(xp * Y, HY)] = (sum_p[:HY] + x_one[0].astype(F32)).astype(BF16)
    x_copies[4].start()
    x_copies[1].wait_recv()
    xs[pl.ds(xm * Y + HY, HY)] = (sum_m[HY:] + x_one[1].astype(F32)).astype(BF16)
    x_copies[5].start()
    y_own[...] = chip_sum(3)

    def relay(i, carry):
        s = rem(z + Z - turn(i), Z)

        @pl.when((core == 1) & (c >= 2))
        def _():
            ahead(0, s, 0).wait_recv()
            across(0, s).start()
            ahead(1, s, 0).wait_recv()
            across(1, s).start()

        return carry

    lax.fori_loop(0, Z, relay, 0)

    for j in range(2, 6):
        x_copies[j].wait_recv()
    y_own[...] = y_own[...] + x_two[0].astype(F32) + x_two[1].astype(F32)
    xs[pl.ds(x * Y, Y)] = y_own[...].astype(BF16)

    def y_copy(d):
        t = rem(y + d, Y)
        return remote(xs.at[x * Y + t], y_in.at[d - 1], y_send.at[d - 1], y_recv.at[d - 1], at(x, t))

    y_order = []
    for d in range(1, Y // 2):
        y_order += [d, Y - d]
    y_order.append(Y // 2)
    for d in y_order:
        y_copy(d).start()

    for d in order:
        z_copy(2, d).wait_recv()
    own_copies[2].wait()

    def arrived(i, carry):
        @pl.when((core == 1) | (c >= 2))
        def _():
            across(0, i).wait_recv()
            across(1, i).wait_recv()

        @pl.when((core == 0) & (c >= 2))
        def _():
            ahead(0, i, 0).wait_recv()
            ahead(1, i, 0).wait_recv()

        return carry

    lax.fori_loop(0, Z, arrived, 0)

    tiles = T // TQ
    units = (F // AHD) * tiles
    span = 2 * T + TQ
    r_at = lax.broadcasted_iota(jnp.int32, (TQ, TQ), 0)
    c_at = lax.broadcasted_iota(jnp.int32, (TQ, TQ), 1)
    after = c_at > r_at
    k_at = lax.broadcasted_iota(jnp.int32, (1, span), 1)
    factor = math.log2(math.e) / math.sqrt(AHD)

    def attend(u, carry):
        head = lax.div(u, tiles)
        start = pl.multiple_of(rem(u, tiles) * TQ, TQ)
        lanes = pl.ds(pl.multiple_of(head * AHD, AHD), AHD)
        keys = pl.ds(start, span)
        rows = pl.ds(start, TQ)
        scores = dot(qbuf[rows, lanes], kbuf[keys, lanes], NT)
        bias = jnp.where(k_at + start >= 2 * T - c * T, 0.0, NEG)
        scores = scores + bias
        first = jnp.where(after, scores[:, :TQ], NEG)
        last = jnp.where(after, NEG, scores[:, 2 * T :])
        scores = jnp.concatenate([first, scores[:, TQ : 2 * T], last], axis=1)
        peak = jnp.max(scores, axis=1, keepdims=True)
        expo = jnp.exp2((scores - peak) * factor)
        total = jnp.sum(expo, axis=1, keepdims=True)
        mixed = dot(expo.astype(BF16), vbuf[keys, lanes], NN)
        attended[rows, lanes] = mixed / total
        return carry

    cut_a, cut_b = units * 5 // 16, units * 10 // 16
    lax.fori_loop(0, cut_a, attend, 0)

    for d in y_order:
        y_copy(d).wait_recv()
    total = y_own[y]
    for d in range(1, Y):
        total = total + y_in[d - 1].astype(F32)
    owner = core * G + x * Y + y
    group = pl.ds(pl.multiple_of(lax.div(owner * 8, 128) * 128, 128), 128)
    inside = pl.multiple_of(rem(owner * 8, 128), 8)
    for m in range(3):
        weights[m, 0:128, :] = weights[m, :, group].T
        before = weights[m, pl.ds(inside, 8), :]
        norm_before = jnp.sqrt(jnp.sum(before * before, axis=1, keepdims=True) + EPS)
        low = before[:, :H] + total[m * 16 : m * 16 + 8]
        high = before[:, H:] + total[m * 16 + 8 : m * 16 + 16]
        squares = jnp.sum(low * low, axis=1, keepdims=True) + jnp.sum(high * high, axis=1, keepdims=True)
        ratio = norm_before / jnp.sqrt(squares + EPS)
        gathered[owner, m * 16 : m * 16 + 16, :] = jnp.concatenate([low * ratio, high * ratio], axis=0).astype(BF16)

    def gy_copy(d):
        return remote(gathered.at[owner], gathered.at[owner], g_send.at[d - 1], g_recv.at[d - 1], at(x, rem(y + d, Y)))

    for d in y_order:
        gy_copy(d).start()
    lax.fori_loop(cut_a, cut_b, attend, 0)
    for d in y_order:
        gy_copy(d).wait_recv()

    def gx_copy(j, xx, lo, n, to):
        group = gathered.at[pl.ds(core * G + xx * Y + lo, n)]
        return remote(group, group, gx_send.at[j], gx_recv.at[j], to)

    def gc_copy(j, xx):
        group = gathered.at[pl.ds(core * G + xx * Y, Y)]
        return remote(group, group, gc_send.at[j], gc_recv.at[j], mate)

    gx = [
        gx_copy(0, x, 0, HY, to_p),
        gx_copy(1, x, HY, HY, to_m),
        gx_copy(2, x, HY, HY, to_p),
        gx_copy(3, x, 0, HY, to_m),
        gx_copy(4, xm, 0, HY, to_p),
        gx_copy(5, xp, HY, HY, to_m),
    ]
    gc = [gc_copy(0, x), gc_copy(1, xm), gc_copy(2, xp), gc_copy(3, xo)]
    for j in range(4):
        gx[j].start()
    gc[0].start()
    gx[0].wait_recv()
    gx[4].start()
    gx[1].wait_recv()
    gx[5].start()
    lax.fori_loop(cut_b, units, attend, 0)
    gx[2].wait_recv()
    gc[1].start()
    gx[3].wait_recv()
    gc[2].start()
    gx[4].wait_recv()
    gx[5].wait_recv()
    gc[3].start()
    for j in range(4):
        gc[j].wait_recv()

    for m in range(3):
        block = gathered[:, m * 16 : m * 16 + 16, :].astype(F32)
        renormed[m, :, :H] = block[:, :8].reshape(F, H).astype(BF16)
        renormed[m, :, H:] = block[:, 8:].reshape(F, H).astype(BF16)

    def read_rows(i, carry):
        rows = pl.ds(pl.multiple_of(i * TQ, TQ), TQ)
        q = qbuf[rows, :]
        gate = dot(q, renormed[0], NT)
        up = dot(q, renormed[1], NT)
        inner = (gate * sigmoid(gate) * up).astype(BF16)
        read = dot(inner, renormed[2], NT)
        scale = lax.rsqrt(jnp.mean(read * read, axis=1, keepdims=True) + RMS_EPS)
        out[rows, :] = (attended[rows, :] + read * scale * gain[...]).astype(BF16)
        return carry

    lax.fori_loop(0, T // TQ, read_rows, 0)

    for d in order:
        for which in range(3):
            z_copy(which, d).wait_send()

    def sent(i, carry):
        @pl.when(c + 2 < C)
        def _():
            ahead(0, i, 0).wait_send()
            ahead(1, i, 0).wait_send()

        @pl.when((core == 0) | (c >= 2))
        def _():
            across(0, i).wait_send()
            across(1, i).wait_send()

        return carry

    lax.fori_loop(0, Z, sent, 0)
    for j in range(4):
        core_copy(j, blocks[j]).wait_send()
    for copy in x_copies + gx + gc:
        copy.wait_send()
    for d in y_order:
        y_copy(d).wait_send()
        gy_copy(d).wait_send()


def solution(mesh):
    C, Z = mesh.shape["ctx"], mesh.shape["head"]
    Y = C // (2 * X)

    def step(queries, keys, values, rates, fast_gate, fast_up, fast_down, out_gain):
        B = queries.shape[0]
        T, F = rates.shape[0], fast_gate.shape[-1]
        H, G = F // 2, X * Y
        dma = pltpu.SemaphoreType.DMA
        vmem = pltpu.VMEM
        any_space = pl.BlockSpec(memory_space=pl.ANY)
        in_vmem = pl.BlockSpec(memory_space=pltpu.VMEM)
        return pl.pallas_call(
            functools.partial(kernel, (Y, Z, T, F, B)),
            out_shape=jax.ShapeDtypeStruct((T, F), BF16),
            in_specs=[any_space] * 3 + [in_vmem] + [any_space] * 3 + [in_vmem],
            out_specs=in_vmem,
            scratch_shapes=[
                vmem((T, F), BF16),
                vmem((3 * T, F), BF16),
                vmem((3 * T, F), BF16),
                vmem((3, F, F), F32),
                vmem((3, F, F), BF16),
                vmem((T, F), BF16),
                vmem((T, F), BF16),
                vmem((T, F), BF16),
                vmem((T, F), BF16),
                vmem((2 * G, 48, H), BF16),
                vmem((G, 48, H), BF16),
                vmem((G, 48, H), BF16),
                vmem((2, Y // 2, 48, H), BF16),
                vmem((2, Y, 48, H), BF16),
                vmem((Y, 48, H), F32),
                vmem((Y - 1, 48, H), BF16),
                vmem((2 * G, 48, H), BF16),
                vmem((3, F, F), BF16),
                vmem((T, F), F32),
                dma((3, Z)),
                dma((3, Z)),
                dma((3,)),
                dma((3,)),
                dma((2, Z)),
                dma((2, Z)),
                dma((2, Z)),
                dma((2, Z)),
                dma((4,)),
                dma((4,)),
                dma((6,)),
                dma((6,)),
                dma((Y - 1,)),
                dma((Y - 1,)),
                dma((Y - 1,)),
                dma((Y - 1,)),
                dma((6,)),
                dma((6,)),
                dma((4,)),
                dma((4,)),
            ],
            compiler_params=pltpu.CompilerParams(
                collective_id=0, has_side_effects=True, vmem_limit_bytes=50 * 1024 * 1024
            ),
        )(
            queries, keys, values, rates,
            fast_gate.reshape(F, F), fast_up.reshape(F, F), fast_down.reshape(F, F), out_gain.reshape(1, F),
        )

    return jax.shard_map(
        step,
        mesh=mesh,
        in_specs=(
            P(("ctx", "head"), None),
            P(("ctx", "head"), None),
            P(("ctx", "head"), None),
            P("ctx", "head"),
            P("head", None, None),
            P("head", None, None),
            P("head", None, None),
            P("head"),
        ),
        out_specs=P("ctx", "head"),
        check_vma=False,
    )
```

```python
import functools
import math

import jax
import jax.numpy as jnp
from jax import lax
from jax.experimental import pallas as pl
from jax.experimental.pallas import tpu as pltpu
from jax.sharding import PartitionSpec as P

AHD = 128
TQ = 128
X = 4
EPS = 1e-06
RMS_EPS = 1e-05
NEG = -1e30
MESH = pl.DeviceIdType.MESH
NT = (((1,), (1,)), ((), ()))
TN = (((0,), (0,)), ((), ()))
NN = (((1,), (0,)), ((), ()))
F32 = jnp.float32
BF16 = jnp.bfloat16


def dot(a, b, dims):
    return lax.dot_general(a, b, dims, preferred_element_type=F32)


def sigmoid(a):
    return 1.0 / (1.0 + jnp.exp(-a))


def kernel(
    sizes,
    q_in, k_in, v_in, rates_in, gate_in, up_in, down_in, gain,
    out,
    stage, qbuf, kv, rates, weights, casts, hidden, target, ggate, gup,
    part, core_in, xs, x_in, y_own, y_in, far_in, hop_out, hop_in, gathered, renormed, attended,
    kv_send, kv_recv, q_send, q_recv, own_sem, in_sem, w_sem, h1_send, h1_recv, h2_send, h2_recv,
    c_send, c_recv, x_send, x_recv, y_send, y_recv, g_send, g_recv, gx_send, gx_recv, gc_send, gc_recv,
):
    Y, Z, T, F, B = sizes
    C = 2 * X * Y
    H = F // 2
    G = X * Y
    rem = lax.rem
    c = lax.axis_index("ctx")
    z = lax.axis_index("head")
    core = rem(c, 2)
    chip = lax.div(c, 2)
    y = rem(chip, Y)
    x = lax.div(chip, Y)
    other = 1 - core
    mate = (c + 1 - 2 * core, z)
    xp, xm, xo = rem(x + 1, X), rem(x + X - 1, X), rem(x + 2, X)

    def at(xx, yy):
        return ((xx * Y + yy) * 2 + core, z)

    def remote(src, dst, send, recv, device):
        return pltpu.make_async_remote_copy(
            src_ref=src, dst_ref=dst, send_sem=send, recv_sem=recv, device_id=device, device_id_type=MESH
        )

    barrier = pltpu.get_barrier_semaphore()
    partners = [(c, rem(z + d, Z)) for d in range(1, Z)]
    partners += [at(xp, y), at(xm, y), at(xo, y), mate]
    partners += [at(x, rem(y + d, Y)) for d in range(1, Y)]
    partners += [(rem(c + 2, C), z), (rem(c + C - 2, C), z)]
    for partner in partners:
        pl.semaphore_signal(barrier, inc=1, device_id=partner, device_id_type=MESH)
    staging = [pltpu.make_async_copy(ref, stage.at[n], in_sem.at[n]) for n, ref in enumerate((k_in, v_in, q_in))]
    loading = [
        pltpu.make_async_copy(ref, weights.at[m], w_sem.at[m]) for m, ref in enumerate((gate_in, up_in, down_in))
    ]
    for copy in staging + loading:
        copy.start()

    pl.semaphore_wait(barrier, len(partners))

    def columns(t):
        return pl.ds(pl.multiple_of(t * F, F), F)

    def kv_copy(d):
        t = rem(z + d, Z)
        rows = pl.ds(2 * T + z * B, B)
        return remote(
            stage.at[pl.ds(0, 2), :, columns(t)], kv.at[:, rows, :], kv_send, kv_recv.at[d], (c, t)
        )

    def q_copy(d):
        t = rem(z + d, Z)
        return remote(
            stage.at[2, :, columns(t)], qbuf.at[pl.ds(z * B, B), :], q_send, q_recv, (c, t)
        )

    order = []
    for d in range(1, Z // 2):
        order += [d, Z - d]
    order.append(Z // 2)
    staging[0].wait()
    staging[1].wait()
    for d in order:
        kv_copy(d).start()
    own_kv = pltpu.make_async_copy(
        stage.at[pl.ds(0, 2), :, columns(z)], kv.at[:, pl.ds(2 * T + z * B, B), :], own_sem.at[0]
    )
    own_kv.start()

    @pl.when(c == 0)
    def _():
        zeros = jnp.zeros((T, F), BF16)
        kv[0, pl.ds(T, T), :] = zeros
        kv[1, pl.ds(T, T), :] = zeros

    @pl.when(c < 2)
    def _():
        zeros = jnp.zeros((T, F), BF16)
        kv[0, pl.ds(0, T), :] = zeros
        kv[1, pl.ds(0, T), :] = zeros

    for copy in loading:
        copy.wait()
    owner = core * G + x * Y + y
    group = pl.ds(pl.multiple_of(lax.div(owner * 8, 128) * 128, 128), 128)
    inside = pl.multiple_of(rem(owner * 8, 128), 8)
    for m in range(3):
        casts[m] = weights[m].astype(BF16)
        weights[m, 0:128, :] = weights[m, :, group].T
    rates[...] = jnp.broadcast_to(rates_in[...], (128, T)).T

    def all_of(ref, send, recv):
        return remote(ref, ref, send, recv, mate)

    def ahead(s):
        return remote(
            kv.at[:, pl.ds(2 * T + s * B, B), :],
            kv.at[:, pl.ds(s * B, B), :],
            h2_send,
            h2_recv,
            (rem(c + 2, C), z),
        )

    all_ahead = all_of(kv.at[:, pl.ds(0, T), :], h2_send, h2_recv)
    across = remote(
        kv.at[:, pl.ds((1 - core) * 2 * T, T), :], kv.at[:, pl.ds(T, T), :], h1_send, h1_recv, mate
    )

    def turn(i):
        return jnp.where(rem(i, 2) == 1, lax.div(i + 1, 2), rem(Z - lax.div(i, 2), Z))

    def update(i, carry):
        d = turn(i)
        s = rem(z + Z - d, Z)

        @pl.when(i == 0)
        def _():
            own_kv.wait()

        @pl.when(i > 0)
        def _():
            kv_copy(d).wait_recv()

        @pl.when(c + 2 < C)
        def _():
            ahead(s).start()

        rows = pl.ds(pl.multiple_of(s * B, B), B)
        here = pl.ds(pl.multiple_of(2 * T + s * B, B), B)
        k = kv[0, here, :]
        rate = jnp.concatenate([rates[rows, :]] * (F // 128), axis=1)
        aim = (rate * kv[1, here, :].astype(F32)).astype(BF16)
        target[rows, :] = aim
        pre_gate = dot(k, casts[0], NN)
        pre_up = dot(k, casts[1], NN)
        back = dot(aim, casts[2], NT)
        sig = sigmoid(pre_gate)
        sil = pre_gate * sig
        hidden[rows, :] = (sil * pre_up).astype(BF16)
        ggate[rows, :] = (back * pre_up * (sig * (1.0 + pre_gate * (1.0 - sig)))).astype(BF16)
        gup[rows, :] = (back * sil).astype(BF16)
        return carry

    lax.fori_loop(0, Z, update, 0)

    staging[2].wait()
    for d in order:
        q_copy(d).start()
    own_q = pltpu.make_async_copy(stage.at[2, :, columns(z)], qbuf.at[pl.ds(z * B, B), :], own_sem.at[1])
    own_q.start()

    here = pl.ds(2 * T, T)

    def packed(step):
        low = step[:, :H].reshape(G, 8, H)
        high = step[:, H:].reshape(G, 8, H)
        return jnp.concatenate([low, high], axis=1).astype(BF16)

    def steps(half):
        cols = pl.ds(pl.multiple_of(half * H, H), H)
        rows = pl.ds(half * G, G)
        part[rows, 0:16, :] = packed(dot(ggate[:, cols], kv[0, here, :], TN))
        part[rows, 16:32, :] = packed(dot(gup[:, cols], kv[0, here, :], TN))
        part[rows, 32:48, :] = packed(dot(target[:, cols], hidden[...], TN))

    blocks = (xp, xm, xo, x)

    def core_copy(j):
        return remote(
            part.at[pl.ds(other * G + blocks[j] * Y, Y)],
            core_in.at[pl.ds(blocks[j] * Y, Y)],
            c_send.at[j],
            c_recv.at[j],
            mate,
        )

    steps(other)
    for j in range(4):
        core_copy(j).start()
    steps(core)

    def chip_sum(j):
        core_copy(j).wait_recv()
        return part[pl.ds(core * G + blocks[j] * Y, Y)].astype(F32) + core_in[pl.ds(blocks[j] * Y, Y)].astype(F32)

    def x_copy(j):
        return remote(xs.at[pl.ds(blocks[j] * Y, Y)], x_in.at[j], x_send.at[j], x_recv.at[j], at(blocks[j], y))

    def y_copy(which, d):
        t = rem(y + d, Y)
        into = (y_in, far_in)[which]
        return remote(
            xs.at[(x, xo)[which] * Y + t], into.at[d - 1], y_send.at[which], y_recv.at[which], at(x, t)
        )

    hop = remote(hop_out, hop_in, x_send.at[2], x_recv.at[2], at(xo, y))
    all_y = all_of(y_in, y_send.at[0], y_recv.at[0])
    all_far = all_of(far_in, y_send.at[1], y_recv.at[1])
    y_order = [Y // 2]
    for d in range(Y // 2 - 1, 0, -1):
        y_order += [d, Y - d]

    for j in range(2):
        xs[pl.ds(blocks[j] * Y, Y)] = chip_sum(j).astype(BF16)
        x_copy(j).start()
    y_own[...] = chip_sum(2)
    far = y_own[y]
    xs[pl.ds(xo * Y, Y)] = y_own[...].astype(BF16)
    for d in y_order:
        y_copy(1, d).start()
    y_own[...] = chip_sum(3)

    @pl.when(core == 0)
    def _():
        across.start()

    for j in range(2):
        x_copy(j).wait_recv()
    y_own[...] = y_own[...] + x_in[0].astype(F32) + x_in[1].astype(F32)
    xs[pl.ds(x * Y, Y)] = y_own[...].astype(BF16)
    for d in y_order:
        y_copy(0, d).start()
    all_far.wait_recv()
    for d in range(1, Y):
        far = far + far_in[d - 1].astype(F32)
    hop_out[...] = far.astype(BF16)
    hop.start()

    @pl.when(c >= 2)
    def _():
        all_ahead.wait_recv()

    @pl.when((core == 1) & (c >= 2))
    def _():
        across.start()

    all_y.wait_recv()
    total = y_own[y]
    for d in range(1, Y):
        total = total + y_in[d - 1].astype(F32)
    hop.wait_recv()
    total = total + hop_in[...].astype(F32)
    for m in range(3):
        before = weights[m, pl.ds(inside, 8), :]
        norm_before = jnp.sqrt(jnp.sum(before * before, axis=1, keepdims=True) + EPS)
        low = before[:, :H] + total[m * 16 : m * 16 + 8]
        high = before[:, H:] + total[m * 16 + 8 : m * 16 + 16]
        squares = jnp.sum(low * low, axis=1, keepdims=True) + jnp.sum(high * high, axis=1, keepdims=True)
        ratio = norm_before / jnp.sqrt(squares + EPS)
        gathered[owner, m * 16 : m * 16 + 16, :] = jnp.concatenate([low * ratio, high * ratio], axis=0).astype(BF16)

    def gy_copy(which, d):
        block = gathered.at[core * G + (x, xo)[which] * Y + y]
        return remote(block, block, g_send.at[which], g_recv.at[which], at(x, rem(y + d, Y)))

    def gx_copy(j):
        group = gathered.at[pl.ds(core * G + x * Y, Y)]
        return remote(group, group, gx_send.at[j], gx_recv.at[j], at(blocks[j], y))

    def gc_copy(j):
        group = gathered.at[pl.ds(core * G + blocks[j] * Y, Y)]
        return remote(group, group, gc_send.at[j], gc_recv.at[j], mate)

    opposite = remote(gathered.at[owner], gathered.at[owner], gx_send.at[2], gx_recv.at[2], at(xo, y))
    seven = gathered.at[pl.ds(0, Y - 1)]
    all_gy = [all_of(seven, g_send.at[which], g_recv.at[which]) for which in range(2)]
    opposite.start()
    for d in y_order:
        gy_copy(0, d).start()

    all_q = all_of(qbuf.at[pl.ds(0, (Z - 1) * B), :], q_send, q_recv)
    all_q.wait_recv()
    own_q.wait()

    @pl.when((core == 1) | (c >= 2))
    def _():
        across.wait_recv()

    tiles = T // TQ
    units = (F // AHD) * tiles
    span = 2 * T + TQ
    r_at = lax.broadcasted_iota(jnp.int32, (TQ, TQ), 0)
    c_at = lax.broadcasted_iota(jnp.int32, (TQ, TQ), 1)
    after = c_at > r_at
    k_at = lax.broadcasted_iota(jnp.int32, (1, span), 1)
    factor = math.log2(math.e) / math.sqrt(AHD)

    def attend(u, carry):
        head = lax.div(u, tiles)
        start = pl.multiple_of(rem(u, tiles) * TQ, TQ)
        lanes = pl.ds(pl.multiple_of(head * AHD, AHD), AHD)
        keys = pl.ds(start, span)
        rows = pl.ds(start, TQ)
        scores = dot(qbuf[rows, lanes], kv[0, keys, lanes], NT)
        bias = jnp.where(k_at + start >= 2 * T - c * T, 0.0, NEG)
        scores = scores + bias
        first = jnp.where(after, scores[:, :TQ], NEG)
        last = jnp.where(after, NEG, scores[:, 2 * T :])
        scores = jnp.concatenate([first, scores[:, TQ : 2 * T], last], axis=1)
        peak = jnp.max(scores, axis=1, keepdims=True)
        expo = jnp.exp2((scores - peak) * factor)
        total = jnp.sum(expo, axis=1, keepdims=True)
        mixed = dot(expo.astype(BF16), kv[1, keys, lanes], NN)
        attended[rows, lanes] = mixed / total
        return carry

    cuts = [units * n // 16 for n in (0, 6, 10, 16)]
    lax.fori_loop(cuts[0], cuts[1], attend, 0)
    opposite.wait_recv()
    for d in y_order:
        gy_copy(1, d).start()
    lax.fori_loop(cuts[1], cuts[2], attend, 0)
    all_gy[0].wait_recv()
    for j in range(2):
        gx_copy(j).start()
    gc_copy(3).start()
    lax.fori_loop(cuts[2], cuts[3], attend, 0)

    all_of(kv.at[:, pl.ds(0, (Z - 1) * B), :], kv_send, h1_recv).wait_send()
    all_q.wait_send()

    @pl.when(c + 2 < C)
    def _():
        all_ahead.wait_send()

    @pl.when((core == 0) | (c >= 2))
    def _():
        across.wait_send()

    for j in range(4):
        core_copy(j).wait_send()
    for j in range(2):
        x_copy(j).wait_send()
    hop.wait_send()
    all_y.wait_send()
    all_far.wait_send()
    opposite.wait_send()
    all_gy[0].wait_send()

    for j in range(2):
        gx_copy(j).wait_recv()
        gc_copy(1 - j).start()
    all_gy[1].wait_recv()
    gc_copy(2).start()

    def unpack(half):
        rows = pl.ds(pl.multiple_of(half * H, H), H)
        for m in range(3):
            block = gathered[pl.ds(half * G, G), m * 16 : m * 16 + 16, :].astype(F32)
            renormed[m, rows, :H] = block[:, :8].reshape(H, H).astype(BF16)
            renormed[m, rows, H:] = block[:, 8:].reshape(H, H).astype(BF16)

    def inner(half):
        cols = pl.ds(pl.multiple_of(half * H, H), H)
        gate = dot(qbuf[...], renormed[0, cols, :], NT)
        up = dot(qbuf[...], renormed[1, cols, :], NT)
        hidden[:, cols] = (gate * sigmoid(gate) * up).astype(BF16)

    unpack(core)
    inner(core)
    for j in range(4):
        gc_copy(j).wait_recv()
    unpack(other)
    inner(other)

    def read_rows(i, carry):
        rows = pl.ds(pl.multiple_of(i * TQ, TQ), TQ)
        read = dot(hidden[rows, :], renormed[2], NT)
        scale = lax.rsqrt(jnp.mean(read * read, axis=1, keepdims=True) + RMS_EPS)
        out[rows, :] = (attended[rows, :] + read * scale * gain[...]).astype(BF16)
        return carry

    lax.fori_loop(0, T // TQ, read_rows, 0)

    all_gy[1].wait_send()
    for j in range(2):
        gx_copy(j).wait_send()
    for j in range(4):
        gc_copy(j).wait_send()


def solution(mesh):
    C, Z = mesh.shape["ctx"], mesh.shape["head"]
    Y = C // (2 * X)

    def step(queries, keys, values, rates, fast_gate, fast_up, fast_down, out_gain):
        B = queries.shape[0]
        T, F = rates.shape[0], fast_gate.shape[-1]
        H, G = F // 2, X * Y
        dma = pltpu.SemaphoreType.DMA
        vmem = pltpu.VMEM
        any_space = pl.BlockSpec(memory_space=pltpu.HBM)
        in_vmem = pl.BlockSpec(memory_space=pltpu.VMEM)
        return pl.pallas_call(
            functools.partial(kernel, (Y, Z, T, F, B)),
            out_shape=jax.ShapeDtypeStruct((T, F), BF16),
            in_specs=[any_space] * 3 + [in_vmem] + [any_space] * 3 + [in_vmem],
            out_specs=in_vmem,
            scratch_shapes=[
                vmem((3, B, Z * F), BF16),
                vmem((T, F), BF16),
                vmem((2, 3 * T, F), BF16),
                vmem((T, 128), F32),
                vmem((3, F, F), F32),
                vmem((3, F, F), BF16),
                vmem((T, F), BF16),
                vmem((T, F), BF16),
                vmem((T, F), BF16),
                vmem((T, F), BF16),
                vmem((2 * G, 48, H), BF16),
                vmem((G, 48, H), BF16),
                vmem((G, 48, H), BF16),
                vmem((2, Y, 48, H), BF16),
                vmem((Y, 48, H), F32),
                vmem((Y - 1, 48, H), BF16),
                vmem((Y - 1, 48, H), BF16),
                vmem((48, H), BF16),
                vmem((48, H), BF16),
                vmem((2 * G, 48, H), BF16),
                vmem((3, F, F), BF16),
                vmem((T, F), F32),
                dma,
                dma((Z,)),
                dma,
                dma,
                dma((2,)),
                dma((3,)),
                dma((3,)),
                dma,
                dma,
                dma,
                dma,
                dma((4,)),
                dma((4,)),
                dma((3,)),
                dma((3,)),
                dma((2,)),
                dma((2,)),
                dma((2,)),
                dma((2,)),
                dma((3,)),
                dma((3,)),
                dma((4,)),
                dma((4,)),
            ],
            compiler_params=pltpu.CompilerParams(
                collective_id=0, has_side_effects=True, vmem_limit_bytes=56 * 1024 * 1024
            ),
        )(
            queries, keys, values, rates.reshape(1, T),
            fast_gate.reshape(F, F), fast_up.reshape(F, F), fast_down.reshape(F, F), out_gain.reshape(1, F),
        )

    return jax.shard_map(
        step,
        mesh=mesh,
        in_specs=(
            P(("ctx", "head"), None),
            P(("ctx", "head"), None),
            P(("ctx", "head"), None),
            P("ctx", "head"),
            P("head", None, None),
            P("head", None, None),
            P("head", None, None),
            P("head"),
        ),
        out_specs=P("ctx", "head"),
        check_vma=False,
    )
```

```python
import functools
import math

import jax
import jax.numpy as jnp
from jax import lax
from jax.experimental import pallas as pl
from jax.experimental.pallas import tpu as pltpu
from jax.sharding import PartitionSpec as P

AHD = 128
TQ = 128
X = 4
EPS = 1e-06
RMS_EPS = 1e-05
NEG = -1e30
MESH = pl.DeviceIdType.MESH
NT = (((1,), (1,)), ((), ()))
TN = (((0,), (0,)), ((), ()))
NN = (((1,), (0,)), ((), ()))
F32 = jnp.float32
BF16 = jnp.bfloat16


def dot(a, b, dims):
    return lax.dot_general(a, b, dims, preferred_element_type=F32)


def sigmoid(a):
    return 1.0 / (1.0 + jnp.exp(-a))


def kernel(
    sizes,
    q_in, k_in, v_in, rates_in, gate_in, up_in, down_in, gain,
    out,
    stage, qbuf, kv, rates, weights, casts, hidden, target, ggate, gup,
    part, core_in, xs, x_in, y_own, y_in, far_in, hop_out, hop_in, gathered, renormed, attended,
    kv_send, kv_recv, q_send, q_recv, own_sem, in_sem, w_sem, h1_send, h1_recv, h2_send, h2_recv,
    c_send, c_recv, hop_send, hop_recv, x_send, x_recv, y_send, y_recv, g_send, g_recv, gx_send, gx_recv, gc_send, gc_recv,
):
    Y, Z, T, F, B = sizes
    C = 2 * X * Y
    H = F // 2
    G = X * Y
    HY = Y // 2
    rem = lax.rem
    c = lax.axis_index("ctx")
    z = lax.axis_index("head")
    core = rem(c, 2)
    chip = lax.div(c, 2)
    y = rem(chip, Y)
    x = lax.div(chip, Y)
    other = 1 - core
    mate = (c + 1 - 2 * core, z)
    xp, xm, xo = rem(x + 1, X), rem(x + X - 1, X), rem(x + 2, X)

    def at(xx, yy):
        return ((xx * Y + yy) * 2 + core, z)

    def remote(src, dst, send, recv, device):
        return pltpu.make_async_remote_copy(
            src_ref=src, dst_ref=dst, send_sem=send, recv_sem=recv, device_id=device, device_id_type=MESH
        )

    barrier = pltpu.get_barrier_semaphore()
    partners = [(c, rem(z + d, Z)) for d in range(1, Z)]
    partners += [at(xp, y), at(xm, y), at(xo, y), mate]
    partners += [at(x, rem(y + d, Y)) for d in range(1, Y)]
    partners += [(rem(c + 2, C), z), (rem(c + C - 2, C), z)]
    for partner in partners:
        pl.semaphore_signal(barrier, inc=1, device_id=partner, device_id_type=MESH)
    staging = [pltpu.make_async_copy(ref, stage.at[n], in_sem.at[n]) for n, ref in enumerate((k_in, v_in, q_in))]
    loading = [
        pltpu.make_async_copy(ref, weights.at[m], w_sem.at[m]) for m, ref in enumerate((gate_in, up_in, down_in))
    ]
    for copy in staging + loading:
        copy.start()

    pl.semaphore_wait(barrier, len(partners))

    def columns(t):
        return pl.ds(pl.multiple_of(t * F, F), F)

    def kv_copy(d):
        t = rem(z + d, Z)
        rows = pl.ds(2 * T + z * B, B)
        return remote(
            stage.at[pl.ds(0, 2), :, columns(t)], kv.at[:, rows, :], kv_send, kv_recv.at[d], (c, t)
        )

    def q_copy(d):
        t = rem(z + d, Z)
        return remote(
            stage.at[2, :, columns(t)], qbuf.at[pl.ds(z * B, B), :], q_send, q_recv, (c, t)
        )

    order = []
    for d in range(1, Z // 2):
        order += [d, Z - d]
    order.append(Z // 2)
    staging[0].wait()
    staging[1].wait()
    for d in order:
        kv_copy(d).start()
    own_kv = pltpu.make_async_copy(
        stage.at[pl.ds(0, 2), :, columns(z)], kv.at[:, pl.ds(2 * T + z * B, B), :], own_sem.at[0]
    )
    own_kv.start()

    @pl.when(c == 0)
    def _():
        zeros = jnp.zeros((T, F), BF16)
        kv[0, pl.ds(T, T), :] = zeros
        kv[1, pl.ds(T, T), :] = zeros

    @pl.when(c < 2)
    def _():
        zeros = jnp.zeros((T, F), BF16)
        kv[0, pl.ds(0, T), :] = zeros
        kv[1, pl.ds(0, T), :] = zeros

    for copy in loading:
        copy.wait()
    owner = core * G + x * Y + y
    group = pl.ds(pl.multiple_of(lax.div(owner * 8, 128) * 128, 128), 128)
    inside = pl.multiple_of(rem(owner * 8, 128), 8)
    for m in range(3):
        casts[m] = weights[m].astype(BF16)
        weights[m, 0:128, :] = weights[m, :, group].T
    rates[...] = jnp.broadcast_to(rates_in[...], (128, T)).T

    def all_of(ref, send, recv):
        return remote(ref, ref, send, recv, mate)

    def ahead(s):
        return remote(
            kv.at[:, pl.ds(2 * T + s * B, B), :],
            kv.at[:, pl.ds(s * B, B), :],
            h2_send,
            h2_recv,
            (rem(c + 2, C), z),
        )

    all_ahead = all_of(kv.at[:, pl.ds(0, T), :], h2_send, h2_recv)
    across = remote(
        kv.at[:, pl.ds((1 - core) * 2 * T, T), :], kv.at[:, pl.ds(T, T), :], h1_send, h1_recv, mate
    )

    def turn(i):
        return jnp.where(rem(i, 2) == 1, lax.div(i + 1, 2), rem(Z - lax.div(i, 2), Z))

    def update(i, carry):
        d = turn(i)
        s = rem(z + Z - d, Z)

        @pl.when(i == 0)
        def _():
            own_kv.wait()

        @pl.when(i > 0)
        def _():
            kv_copy(d).wait_recv()

        @pl.when(c + 2 < C)
        def _():
            ahead(s).start()

        rows = pl.ds(pl.multiple_of(s * B, B), B)
        here = pl.ds(pl.multiple_of(2 * T + s * B, B), B)
        k = kv[0, here, :]
        rate = jnp.concatenate([rates[rows, :]] * (F // 128), axis=1)
        aim = (rate * kv[1, here, :].astype(F32)).astype(BF16)
        target[rows, :] = aim
        pre_gate = dot(k, casts[0], NN)
        pre_up = dot(k, casts[1], NN)
        back = dot(aim, casts[2], NT)
        sig = sigmoid(pre_gate)
        sil = pre_gate * sig
        hidden[rows, :] = (sil * pre_up).astype(BF16)
        ggate[rows, :] = (back * pre_up * (sig * (1.0 + pre_gate * (1.0 - sig)))).astype(BF16)
        gup[rows, :] = (back * sil).astype(BF16)
        return carry

    lax.fori_loop(0, Z, update, 0)

    staging[2].wait()
    for d in order:
        q_copy(d).start()
    own_q = pltpu.make_async_copy(stage.at[2, :, columns(z)], qbuf.at[pl.ds(z * B, B), :], own_sem.at[1])
    own_q.start()

    here = pl.ds(2 * T, T)

    def packed(step):
        low = step[:, :H].reshape(G, 8, H)
        high = step[:, H:].reshape(G, 8, H)
        return jnp.concatenate([low, high], axis=1).astype(BF16)

    def steps(half):
        cols = pl.ds(pl.multiple_of(half * H, H), H)
        rows = pl.ds(half * G, G)
        part[rows, 0:16, :] = packed(dot(ggate[:, cols], kv[0, here, :], TN))
        part[rows, 16:32, :] = packed(dot(gup[:, cols], kv[0, here, :], TN))
        part[rows, 32:48, :] = packed(dot(target[:, cols], hidden[...], TN))

    blocks = (xp, xm, xo, x)

    def core_copy(j):
        return remote(
            part.at[pl.ds(other * G + blocks[j] * Y, Y)],
            core_in.at[pl.ds(blocks[j] * Y, Y)],
            c_send.at[j],
            c_recv.at[j],
            mate,
        )

    steps(other)
    for j in range(4):
        core_copy(j).start()
    steps(core)

    def chip_sum(j):
        core_copy(j).wait_recv()
        return part[pl.ds(core * G + blocks[j] * Y, Y)].astype(F32) + core_in[pl.ds(blocks[j] * Y, Y)].astype(F32)

    def half_of(xx, side):
        return pl.ds(xx * Y + side * HY, HY)

    def x_copy(j, side):
        return remote(
            xs.at[half_of(blocks[j], side)],
            x_in.at[j, pl.ds(side * HY, HY)],
            x_send.at[j, side],
            x_recv.at[j, side],
            at(blocks[j], y),
        )

    def y_copy(which, t):
        into = (y_in, far_in)[which]
        return remote(
            xs.at[(x, xo)[which] * Y + t],
            into.at[rem(t - y + Y, Y) - 1],
            y_send.at[which],
            y_recv.at[which],
            at(x, t),
        )

    hop = remote(hop_out, hop_in, hop_send.at[0], hop_recv.at[0], at(xo, y))
    all_y = all_of(y_in, y_send.at[0], y_recv.at[0])
    all_far = all_of(far_in, y_send.at[1], y_recv.at[1])
    near = lax.div(y, HY)
    sides = (1 - near, near)
    others = [(1 - near) * HY + e for e in range(HY)]
    close = [near * HY + rem(y + e, HY) for e in range(1, HY)]

    for j in range(2):
        xs[pl.ds(blocks[j] * Y, Y)] = chip_sum(j).astype(BF16)
        x_copy(j, sides[0]).start()
    for j in range(2):
        x_copy(j, sides[1]).start()
    y_own[...] = chip_sum(2)
    far = y_own[y]
    xs[pl.ds(xo * Y, Y)] = y_own[...].astype(BF16)
    for t in others + close:
        y_copy(1, t).start()
    y_own[...] = chip_sum(3)

    @pl.when(core == 0)
    def _():
        across.start()

    for side, peers in zip(sides, (others, close)):
        rows = pl.ds(side * HY, HY)
        for j in range(2):
            x_copy(j, side).wait_recv()
        y_own[rows] = y_own[rows] + x_in[0, rows].astype(F32) + x_in[1, rows].astype(F32)
        xs[half_of(x, side)] = y_own[rows].astype(BF16)
        for t in peers:
            y_copy(0, t).start()
    all_far.wait_recv()
    for d in range(1, Y):
        far = far + far_in[d - 1].astype(F32)
    hop_out[...] = far.astype(BF16)
    hop.start()

    @pl.when(c >= 2)
    def _():
        all_ahead.wait_recv()

    @pl.when((core == 1) & (c >= 2))
    def _():
        across.start()

    all_y.wait_recv()
    total = y_own[y]
    for d in range(1, Y):
        total = total + y_in[d - 1].astype(F32)
    hop.wait_recv()
    hop.wait_send()
    total = total + hop_in[...].astype(F32)
    for m in range(3):
        before = weights[m, pl.ds(inside, 8), :]
        norm_before = jnp.sqrt(jnp.sum(before * before, axis=1, keepdims=True) + EPS)
        low = before[:, :H] + total[m * 16 : m * 16 + 8]
        high = before[:, H:] + total[m * 16 + 8 : m * 16 + 16]
        squares = jnp.sum(low * low, axis=1, keepdims=True) + jnp.sum(high * high, axis=1, keepdims=True)
        ratio = norm_before / jnp.sqrt(squares + EPS)
        gathered[owner, m * 16 : m * 16 + 16, :] = jnp.concatenate([low * ratio, high * ratio], axis=0).astype(BF16)

    def gy_copy(which, t, sem):
        block = gathered.at[core * G + (x, xo)[which] * Y + y]
        return remote(block, block, g_send.at[sem], g_recv.at[sem], at(x, t))

    def gx_copy(j, side):
        group = gathered.at[pl.ds(core * G + x * Y + side * HY, HY)]
        return remote(group, group, gx_send.at[j, side], gx_recv.at[j, side], at(blocks[j], y))

    def gc_copy(j):
        group = gathered.at[pl.ds(core * G + blocks[j] * Y, Y)]
        return remote(group, group, gc_send.at[j], gc_recv.at[j], mate)

    opposite = remote(gathered.at[owner], gathered.at[owner], hop_send.at[1], hop_recv.at[1], at(xo, y))
    all_gy = [
        all_of(gathered.at[pl.ds(0, n)], g_send.at[sem], g_recv.at[sem]) for sem, n in enumerate((HY - 1, HY, Y - 1))
    ]
    opposite.start()
    for t in close:
        gy_copy(0, t, 0).start()
    for t in others:
        gy_copy(0, t, 1).start()

    all_q = all_of(qbuf.at[pl.ds(0, (Z - 1) * B), :], q_send, q_recv)
    all_q.wait_recv()
    own_q.wait()

    @pl.when((core == 1) | (c >= 2))
    def _():
        across.wait_recv()

    tiles = T // TQ
    units = (F // AHD) * tiles
    span = 2 * T + TQ
    r_at = lax.broadcasted_iota(jnp.int32, (TQ, TQ), 0)
    c_at = lax.broadcasted_iota(jnp.int32, (TQ, TQ), 1)
    after = c_at > r_at
    k_at = lax.broadcasted_iota(jnp.int32, (1, span), 1)
    factor = math.log2(math.e) / math.sqrt(AHD)

    def attend(u, carry):
        head = lax.div(u, tiles)
        start = pl.multiple_of(rem(u, tiles) * TQ, TQ)
        lanes = pl.ds(pl.multiple_of(head * AHD, AHD), AHD)
        keys = pl.ds(start, span)
        rows = pl.ds(start, TQ)
        scores = dot(qbuf[rows, lanes], kv[0, keys, lanes], NT)
        bias = jnp.where(k_at + start >= 2 * T - c * T, 0.0, NEG)
        scores = scores + bias
        first = jnp.where(after, scores[:, :TQ], NEG)
        last = jnp.where(after, NEG, scores[:, 2 * T :])
        scores = jnp.concatenate([first, scores[:, TQ : 2 * T], last], axis=1)
        peak = jnp.max(scores, axis=1, keepdims=True)
        expo = jnp.exp2((scores - peak) * factor)
        total = jnp.sum(expo, axis=1, keepdims=True)
        mixed = dot(expo.astype(BF16), kv[1, keys, lanes], NN)
        attended[rows, lanes] = mixed / total
        return carry

    cuts = [units * n // 16 for n in (0, 5, 8, 9, 16)]
    lax.fori_loop(cuts[0], cuts[1], attend, 0)
    opposite.wait_recv()
    for t in others + close:
        gy_copy(1, t, 2).start()
    lax.fori_loop(cuts[1], cuts[2], attend, 0)
    all_gy[0].wait_recv()
    for j in range(2):
        gx_copy(j, near).start()
    lax.fori_loop(cuts[2], cuts[3], attend, 0)
    all_gy[1].wait_recv()
    for j in range(2):
        gx_copy(j, 1 - near).start()
    gc_copy(3).start()
    lax.fori_loop(cuts[3], cuts[4], attend, 0)

    all_of(kv.at[:, pl.ds(0, (Z - 1) * B), :], kv_send, h1_recv).wait_send()
    all_q.wait_send()

    @pl.when(c + 2 < C)
    def _():
        all_ahead.wait_send()

    @pl.when((core == 0) | (c >= 2))
    def _():
        across.wait_send()

    for j in range(4):
        core_copy(j).wait_send()
    for j in range(2):
        for side in range(2):
            x_copy(j, side).wait_send()
    all_y.wait_send()
    all_far.wait_send()
    opposite.wait_send()
    all_gy[0].wait_send()
    all_gy[1].wait_send()

    for j in range(2):
        for side in sides:
            gx_copy(j, side).wait_recv()
        gc_copy(1 - j).start()
    all_gy[2].wait_recv()
    gc_copy(2).start()

    def unpack(half):
        rows = pl.ds(pl.multiple_of(half * H, H), H)
        for m in range(3):
            block = gathered[pl.ds(half * G, G), m * 16 : m * 16 + 16, :].astype(F32)
            renormed[m, rows, :H] = block[:, :8].reshape(H, H).astype(BF16)
            renormed[m, rows, H:] = block[:, 8:].reshape(H, H).astype(BF16)

    def inner(half):
        cols = pl.ds(pl.multiple_of(half * H, H), H)
        gate = dot(qbuf[...], renormed[0, cols, :], NT)
        up = dot(qbuf[...], renormed[1, cols, :], NT)
        hidden[:, cols] = (gate * sigmoid(gate) * up).astype(BF16)

    unpack(core)
    inner(core)
    for j in range(4):
        gc_copy(j).wait_recv()
    unpack(other)
    inner(other)

    def read_rows(i, carry):
        rows = pl.ds(pl.multiple_of(i * TQ, TQ), TQ)
        read = dot(hidden[rows, :], renormed[2], NT)
        scale = lax.rsqrt(jnp.mean(read * read, axis=1, keepdims=True) + RMS_EPS)
        out[rows, :] = (attended[rows, :] + read * scale * gain[...]).astype(BF16)
        return carry

    lax.fori_loop(0, T // TQ, read_rows, 0)

    all_gy[2].wait_send()
    for j in range(2):
        for side in range(2):
            gx_copy(j, side).wait_send()
    for j in range(4):
        gc_copy(j).wait_send()


def solution(mesh):
    C, Z = mesh.shape["ctx"], mesh.shape["head"]
    Y = C // (2 * X)

    def step(queries, keys, values, rates, fast_gate, fast_up, fast_down, out_gain):
        B = queries.shape[0]
        T, F = rates.shape[0], fast_gate.shape[-1]
        H, G = F // 2, X * Y
        dma = pltpu.SemaphoreType.DMA
        vmem = pltpu.VMEM
        any_space = pl.BlockSpec(memory_space=pltpu.HBM)
        in_vmem = pl.BlockSpec(memory_space=pltpu.VMEM)
        return pl.pallas_call(
            functools.partial(kernel, (Y, Z, T, F, B)),
            out_shape=jax.ShapeDtypeStruct((T, F), BF16),
            in_specs=[any_space] * 3 + [in_vmem] + [any_space] * 3 + [in_vmem],
            out_specs=in_vmem,
            scratch_shapes=[
                vmem((3, B, Z * F), BF16),
                vmem((T, F), BF16),
                vmem((2, 3 * T, F), BF16),
                vmem((T, 128), F32),
                vmem((3, F, F), F32),
                vmem((3, F, F), BF16),
                vmem((T, F), BF16),
                vmem((T, F), BF16),
                vmem((T, F), BF16),
                vmem((T, F), BF16),
                vmem((2 * G, 48, H), BF16),
                vmem((G, 48, H), BF16),
                vmem((G, 48, H), BF16),
                vmem((2, Y, 48, H), BF16),
                vmem((Y, 48, H), F32),
                vmem((Y - 1, 48, H), BF16),
                vmem((Y - 1, 48, H), BF16),
                vmem((48, H), BF16),
                vmem((48, H), BF16),
                vmem((2 * G, 48, H), BF16),
                vmem((3, F, F), BF16),
                vmem((T, F), F32),
                dma,
                dma((Z,)),
                dma,
                dma,
                dma((2,)),
                dma((3,)),
                dma((3,)),
                dma,
                dma,
                dma,
                dma,
                dma((4,)),
                dma((4,)),
                dma((2,)),
                dma((2,)),
                dma((2, 2)),
                dma((2, 2)),
                dma((2,)),
                dma((2,)),
                dma((3,)),
                dma((3,)),
                dma((2, 2)),
                dma((2, 2)),
                dma((4,)),
                dma((4,)),
            ],
            compiler_params=pltpu.CompilerParams(
                collective_id=0, has_side_effects=True, vmem_limit_bytes=54640 * 1024
            ),
        )(
            queries, keys, values, rates.reshape(1, T),
            fast_gate.reshape(F, F), fast_up.reshape(F, F), fast_down.reshape(F, F), out_gain.reshape(1, F),
        )

    return jax.shard_map(
        step,
        mesh=mesh,
        in_specs=(
            P(("ctx", "head"), None),
            P(("ctx", "head"), None),
            P(("ctx", "head"), None),
            P("ctx", "head"),
            P("head", None, None),
            P("head", None, None),
            P("head", None, None),
            P("head"),
        ),
        out_specs=P("ctx", "head"),
        check_vma=False,
    )
```

```python
import functools
import math

import jax
import jax.numpy as jnp
from jax import lax
from jax.experimental import pallas as pl
from jax.experimental.pallas import tpu as pltpu
from jax.sharding import PartitionSpec as P

AHD = 128
TQ = 256
X = 4
EPS = 1e-06
RMS_EPS = 1e-05
NEG = -1e30
MESH = pl.DeviceIdType.MESH
NT = (((1,), (1,)), ((), ()))
TN = (((0,), (0,)), ((), ()))
NN = (((1,), (0,)), ((), ()))
F32 = jnp.float32
BF16 = jnp.bfloat16


def dot(a, b, dims):
    return lax.dot_general(a, b, dims, preferred_element_type=F32)


def sigmoid(a):
    return 1.0 / (1.0 + jnp.exp(-a))


def kernel(
    sizes,
    q_in, k_in, v_in, rates_in, gate_in, up_in, down_in, gain_in,
    out,
    stage, qbuf, kv, rate_row, gain, rates, weights, casts, hidden, target, ggate, gup,
    part, core_in, xs, x_in, y_own, y_in, far_in, hop_out, hop_in, gathered, renormed, attended,
    kv_send, kv_recv, q_send, q_recv, own_sem, in_sem, w_sem, h1_send, h1_recv, h2_send, h2_recv,
    c_send, c_recv, hop_send, hop_recv, x_send, x_recv, y_send, y_recv, g_send, g_recv, gx_send, gx_recv, gc_send, gc_recv,
):
    Y, Z, T, F, B = sizes
    C = 2 * X * Y
    H = F // 2
    G = X * Y
    HY = Y // 2
    rem = lax.rem
    c = lax.axis_index("ctx")
    z = lax.axis_index("head")
    core = rem(c, 2)
    chip = lax.div(c, 2)
    y = rem(chip, Y)
    x = lax.div(chip, Y)
    other = 1 - core
    mate = (c + 1 - 2 * core, z)
    xp, xm, xo = rem(x + 1, X), rem(x + X - 1, X), rem(x + 2, X)

    def at(xx, yy):
        return ((xx * Y + yy) * 2 + core, z)

    def remote(src, dst, send, recv, device):
        return pltpu.make_async_remote_copy(
            src_ref=src, dst_ref=dst, send_sem=send, recv_sem=recv, device_id=device, device_id_type=MESH
        )

    staging = [pltpu.make_async_copy(ref, stage.at[n], in_sem.at[n]) for n, ref in enumerate((k_in, v_in, q_in))]
    sources = ((gate_in, weights.at[0]), (up_in, weights.at[1]), (down_in, weights.at[2]), (rates_in, rate_row), (gain_in, gain))
    loading = [pltpu.make_async_copy(src, dst, w_sem.at[m]) for m, (src, dst) in enumerate(sources)]
    staging[0].start()
    staging[1].start()
    barrier = pltpu.get_barrier_semaphore()
    partners = [(c, rem(z + d, Z)) for d in range(1, Z)]
    partners += [at(xp, y), at(xm, y), at(xo, y), mate]
    partners += [at(x, rem(y + d, Y)) for d in range(1, Y)]
    partners += [(rem(c + 2, C), z), (rem(c + C - 2, C), z)]
    for partner in partners:
        pl.semaphore_signal(barrier, inc=1, device_id=partner, device_id_type=MESH)
    for copy in loading + staging[2:]:
        copy.start()
    pl.semaphore_wait(barrier, len(partners))

    def columns(t):
        return pl.ds(pl.multiple_of(t * F, F), F)

    def kv_copy(d):
        t = rem(z + d, Z)
        rows = pl.ds(2 * T + z * B, B)
        return remote(
            stage.at[pl.ds(0, 2), :, columns(t)], kv.at[:, rows, :], kv_send, kv_recv.at[d], (c, t)
        )

    def q_copy(d):
        t = rem(z + d, Z)
        return remote(
            stage.at[2, :, columns(t)], qbuf.at[pl.ds(z * B, B), :], q_send, q_recv, (c, t)
        )

    order = []
    for d in range(1, Z // 2):
        order += [d, Z - d]
    order.append(Z // 2)
    staging[0].wait()
    staging[1].wait()
    for d in order:
        kv_copy(d).start()
    own_kv = pltpu.make_async_copy(
        stage.at[pl.ds(0, 2), :, columns(z)], kv.at[:, pl.ds(2 * T + z * B, B), :], own_sem.at[0]
    )
    own_kv.start()

    @pl.when(c == 0)
    def _():
        zeros = jnp.zeros((T, F), BF16)
        kv[0, pl.ds(T, T), :] = zeros
        kv[1, pl.ds(T, T), :] = zeros

    @pl.when(c < 2)
    def _():
        zeros = jnp.zeros((T, F), BF16)
        kv[0, pl.ds(0, T), :] = zeros
        kv[1, pl.ds(0, T), :] = zeros

    for copy in loading:
        copy.wait()
    owner = core * G + x * Y + y
    group = pl.ds(pl.multiple_of(lax.div(owner * 8, 128) * 128, 128), 128)
    inside = pl.multiple_of(rem(owner * 8, 128), 8)
    for m in range(3):
        casts[m] = weights[m].astype(BF16)
        weights[m, 0:128, :] = weights[m, :, group].T
    rates[...] = jnp.broadcast_to(rate_row[...], (128, T)).T

    def all_of(ref, send, recv):
        return remote(ref, ref, send, recv, mate)

    def ahead(s):
        return remote(
            kv.at[:, pl.ds(2 * T + s * B, B), :],
            kv.at[:, pl.ds(s * B, B), :],
            h2_send,
            h2_recv,
            (rem(c + 2, C), z),
        )

    all_ahead = all_of(kv.at[:, pl.ds(0, T), :], h2_send, h2_recv)
    across = remote(
        kv.at[:, pl.ds((1 - core) * 2 * T, T), :], kv.at[:, pl.ds(T, T), :], h1_send, h1_recv, mate
    )

    def turn(i):
        return jnp.where(rem(i, 2) == 1, lax.div(i + 1, 2), rem(Z - lax.div(i, 2), Z))

    def update(i, carry):
        d = turn(i)
        s = rem(z + Z - d, Z)

        @pl.when(i == 0)
        def _():
            own_kv.wait()

        @pl.when(i > 0)
        def _():
            kv_copy(d).wait_recv()

        @pl.when(c + 2 < C)
        def _():
            ahead(s).start()

        rows = pl.ds(pl.multiple_of(s * B, B), B)
        here = pl.ds(pl.multiple_of(2 * T + s * B, B), B)
        k = kv[0, here, :]
        rate = jnp.concatenate([rates[rows, :]] * (F // 128), axis=1)
        aim = (rate * kv[1, here, :].astype(F32)).astype(BF16)
        target[rows, :] = aim
        pre_gate = dot(k, casts[0], NN)
        pre_up = dot(k, casts[1], NN)
        back = dot(aim, casts[2], NT)
        sig = sigmoid(pre_gate)
        sil = pre_gate * sig
        hidden[rows, :] = (sil * pre_up).astype(BF16)
        ggate[rows, :] = (back * pre_up * (sig * (1.0 + pre_gate * (1.0 - sig)))).astype(BF16)
        gup[rows, :] = (back * sil).astype(BF16)
        return carry

    lax.fori_loop(0, Z, update, 0)

    staging[2].wait()
    for d in order:
        q_copy(d).start()
    own_q = pltpu.make_async_copy(stage.at[2, :, columns(z)], qbuf.at[pl.ds(z * B, B), :], own_sem.at[1])
    own_q.start()

    here = pl.ds(2 * T, T)

    def packed(step):
        low = step[:, :H].reshape(G, 8, H)
        high = step[:, H:].reshape(G, 8, H)
        return jnp.concatenate([low, high], axis=1).astype(BF16)

    def steps(half):
        cols = pl.ds(pl.multiple_of(half * H, H), H)
        rows = pl.ds(half * G, G)
        part[rows, 0:16, :] = packed(dot(ggate[:, cols], kv[0, here, :], TN))
        part[rows, 16:32, :] = packed(dot(gup[:, cols], kv[0, here, :], TN))
        part[rows, 32:48, :] = packed(dot(target[:, cols], hidden[...], TN))

    blocks = (xp, xm, xo, x)

    def core_copy(j):
        return remote(
            part.at[pl.ds(other * G + blocks[j] * Y, Y)],
            core_in.at[pl.ds(blocks[j] * Y, Y)],
            c_send.at[j],
            c_recv.at[j],
            mate,
        )

    steps(other)
    for j in range(4):
        core_copy(j).start()
    steps(core)

    def chip_sum(j):
        core_copy(j).wait_recv()
        return part[pl.ds(core * G + blocks[j] * Y, Y)].astype(F32) + core_in[pl.ds(blocks[j] * Y, Y)].astype(F32)

    def half_of(xx, side):
        return pl.ds(xx * Y + side * HY, HY)

    def x_copy(j, side):
        return remote(
            xs.at[half_of(blocks[j], side)],
            x_in.at[j, pl.ds(side * HY, HY)],
            x_send.at[j, side],
            x_recv.at[j, side],
            at(blocks[j], y),
        )

    def y_copy(which, t):
        into = (y_in, far_in)[which]
        return remote(
            xs.at[(x, xo)[which] * Y + t],
            into.at[rem(t - y + Y, Y) - 1],
            y_send.at[which],
            y_recv.at[which],
            at(x, t),
        )

    hop = remote(hop_out, hop_in, hop_send.at[0], hop_recv.at[0], at(xo, y))
    all_y = all_of(y_in, y_send.at[0], y_recv.at[0])
    all_far = all_of(far_in, y_send.at[1], y_recv.at[1])
    near = lax.div(y, HY)
    sides = (1 - near, near)
    others = [(1 - near) * HY + e for e in range(HY)]
    close = [near * HY + rem(y + e, HY) for e in range(1, HY)]

    for j in range(2):
        xs[pl.ds(blocks[j] * Y, Y)] = chip_sum(j).astype(BF16)
        x_copy(j, sides[0]).start()
    for j in range(2):
        x_copy(j, sides[1]).start()
    y_own[...] = chip_sum(2)
    far = y_own[y]
    xs[pl.ds(xo * Y, Y)] = y_own[...].astype(BF16)
    for t in others + close:
        y_copy(1, t).start()
    y_own[...] = chip_sum(3)

    @pl.when(core == 0)
    def _():
        across.start()

    for side, peers in zip(sides, (others, close)):
        rows = pl.ds(side * HY, HY)
        for j in range(2):
            x_copy(j, side).wait_recv()
        y_own[rows] = y_own[rows] + x_in[0, rows].astype(F32) + x_in[1, rows].astype(F32)
        xs[half_of(x, side)] = y_own[rows].astype(BF16)
        for t in peers:
            y_copy(0, t).start()
    all_far.wait_recv()
    for d in range(1, Y):
        far = far + far_in[d - 1].astype(F32)
    hop_out[...] = far.astype(BF16)
    hop.start()

    @pl.when(c >= 2)
    def _():
        all_ahead.wait_recv()

    @pl.when((core == 1) & (c >= 2))
    def _():
        across.start()

    all_y.wait_recv()
    total = y_own[y]
    for d in range(1, Y):
        total = total + y_in[d - 1].astype(F32)
    hop.wait_recv()
    hop.wait_send()
    total = total + hop_in[...].astype(F32)
    for m in range(3):
        before = weights[m, pl.ds(inside, 8), :]
        norm_before = jnp.sqrt(jnp.sum(before * before, axis=1, keepdims=True) + EPS)
        low = before[:, :H] + total[m * 16 : m * 16 + 8]
        high = before[:, H:] + total[m * 16 + 8 : m * 16 + 16]
        squares = jnp.sum(low * low, axis=1, keepdims=True) + jnp.sum(high * high, axis=1, keepdims=True)
        ratio = norm_before / jnp.sqrt(squares + EPS)
        gathered[owner, m * 16 : m * 16 + 16, :] = jnp.concatenate([low * ratio, high * ratio], axis=0).astype(BF16)

    def gy_copy(which, t, sem):
        block = gathered.at[core * G + (x, xo)[which] * Y + y]
        return remote(block, block, g_send.at[sem], g_recv.at[sem], at(x, t))

    def gx_copy(j, side):
        group = gathered.at[pl.ds(core * G + x * Y + side * HY, HY)]
        return remote(group, group, gx_send.at[j, side], gx_recv.at[j, side], at(blocks[j], y))

    def gc_copy(j):
        group = gathered.at[pl.ds(core * G + blocks[j] * Y, Y)]
        return remote(group, group, gc_send.at[j], gc_recv.at[j], mate)

    opposite = remote(gathered.at[owner], gathered.at[owner], hop_send.at[1], hop_recv.at[1], at(xo, y))
    all_gy = [
        all_of(gathered.at[pl.ds(0, n)], g_send.at[sem], g_recv.at[sem]) for sem, n in enumerate((HY - 1, HY, Y - 1))
    ]
    opposite.start()
    for t in close:
        gy_copy(0, t, 0).start()
    for t in others:
        gy_copy(0, t, 1).start()

    all_q = all_of(qbuf.at[pl.ds(0, (Z - 1) * B), :], q_send, q_recv)
    all_q.wait_recv()
    own_q.wait()

    @pl.when((core == 1) | (c >= 2))
    def _():
        across.wait_recv()

    tiles = T // TQ
    units = (F // AHD) * tiles
    span = 2 * T + TQ
    r_at = lax.broadcasted_iota(jnp.int32, (TQ, TQ), 0)
    c_at = lax.broadcasted_iota(jnp.int32, (TQ, TQ), 1)
    after = c_at > r_at
    k_at = lax.broadcasted_iota(jnp.int32, (1, span), 1)
    factor = math.log2(math.e) / math.sqrt(AHD)

    def attend(u, carry):
        head = lax.div(u, tiles)
        start = pl.multiple_of(rem(u, tiles) * TQ, TQ)
        lanes = pl.ds(pl.multiple_of(head * AHD, AHD), AHD)
        keys = pl.ds(start, span)
        rows = pl.ds(start, TQ)
        scores = dot(qbuf[rows, lanes], kv[0, keys, lanes], NT)
        bias = jnp.where(k_at + start >= 2 * T - c * T, 0.0, NEG)
        scores = scores + bias
        first = jnp.where(after, scores[:, :TQ], NEG)
        last = jnp.where(after, NEG, scores[:, 2 * T :])
        scores = jnp.concatenate([first, scores[:, TQ : 2 * T], last], axis=1)
        peak = jnp.max(scores, axis=1, keepdims=True)
        expo = jnp.exp2((scores - peak) * factor)
        total = jnp.sum(expo, axis=1, keepdims=True)
        mixed = dot(expo.astype(BF16), kv[1, keys, lanes], NN)
        attended[rows, lanes] = mixed / total
        return carry

    cuts = [units * n // 16 for n in (0, 6, 8, 10, 16)]
    lax.fori_loop(cuts[0], cuts[1], attend, 0)
    opposite.wait_recv()
    for t in others + close:
        gy_copy(1, t, 2).start()
    lax.fori_loop(cuts[1], cuts[2], attend, 0)
    all_gy[0].wait_recv()
    for j in range(2):
        gx_copy(j, near).start()
    lax.fori_loop(cuts[2], cuts[3], attend, 0)
    all_gy[1].wait_recv()
    for j in range(2):
        gx_copy(j, 1 - near).start()
    gc_copy(3).start()
    lax.fori_loop(cuts[3], cuts[4], attend, 0)

    all_of(kv.at[:, pl.ds(0, (Z - 1) * B), :], kv_send, h1_recv).wait_send()
    all_q.wait_send()

    @pl.when(c + 2 < C)
    def _():
        all_ahead.wait_send()

    @pl.when((core == 0) | (c >= 2))
    def _():
        across.wait_send()

    for j in range(4):
        core_copy(j).wait_send()
    for j in range(2):
        for side in range(2):
            x_copy(j, side).wait_send()
    all_y.wait_send()
    all_far.wait_send()
    opposite.wait_send()
    all_gy[0].wait_send()
    all_gy[1].wait_send()

    for j in range(2):
        for side in sides:
            gx_copy(j, side).wait_recv()
        gc_copy(1 - j).start()
    all_gy[2].wait_recv()
    gc_copy(2).start()

    def unpack(half):
        rows = pl.ds(pl.multiple_of(half * H, H), H)
        for m in range(3):
            block = gathered[pl.ds(half * G, G), m * 16 : m * 16 + 16, :].astype(F32)
            renormed[m, rows, :H] = block[:, :8].reshape(H, H).astype(BF16)
            renormed[m, rows, H:] = block[:, 8:].reshape(H, H).astype(BF16)

    def inner(half):
        cols = pl.ds(pl.multiple_of(half * H, H), H)
        gate = dot(qbuf[...], renormed[0, cols, :], NT)
        up = dot(qbuf[...], renormed[1, cols, :], NT)
        hidden[:, cols] = (gate * sigmoid(gate) * up).astype(BF16)

    unpack(core)
    inner(core)
    for j in range(4):
        gc_copy(j).wait_recv()
    unpack(other)
    inner(other)

    def read_rows(i, carry):
        rows = pl.ds(pl.multiple_of(i * TQ, TQ), TQ)
        read = dot(hidden[rows, :], renormed[2], NT)
        scale = lax.rsqrt(jnp.mean(read * read, axis=1, keepdims=True) + RMS_EPS)
        out[rows, :] = (attended[rows, :] + read * scale * gain[...]).astype(BF16)
        return carry

    lax.fori_loop(0, T // TQ, read_rows, 0)

    all_gy[2].wait_send()
    for j in range(2):
        for side in range(2):
            gx_copy(j, side).wait_send()
    for j in range(4):
        gc_copy(j).wait_send()


def solution(mesh):
    C, Z = mesh.shape["ctx"], mesh.shape["head"]
    Y = C // (2 * X)

    def step(queries, keys, values, rates, fast_gate, fast_up, fast_down, out_gain):
        B = queries.shape[0]
        T, F = rates.shape[0], fast_gate.shape[-1]
        H, G = F // 2, X * Y
        dma = pltpu.SemaphoreType.DMA
        vmem = pltpu.VMEM
        any_space = pl.BlockSpec(memory_space=pltpu.HBM)
        in_vmem = pl.BlockSpec(memory_space=pltpu.VMEM)
        return pl.pallas_call(
            functools.partial(kernel, (Y, Z, T, F, B)),
            out_shape=jax.ShapeDtypeStruct((T, F), BF16),
            in_specs=[any_space] * 8,
            out_specs=in_vmem,
            scratch_shapes=[
                vmem((3, B, Z * F), BF16),
                vmem((T, F), BF16),
                vmem((2, 3 * T, F), BF16),
                vmem((1, T), F32),
                vmem((1, F), F32),
                vmem((T, 128), F32),
                vmem((3, F, F), F32),
                vmem((3, F, F), BF16),
                vmem((T, F), BF16),
                vmem((T, F), BF16),
                vmem((T, F), BF16),
                vmem((T, F), BF16),
                vmem((2 * G, 48, H), BF16),
                vmem((G, 48, H), BF16),
                vmem((G, 48, H), BF16),
                vmem((2, Y, 48, H), BF16),
                vmem((Y, 48, H), F32),
                vmem((Y - 1, 48, H), BF16),
                vmem((Y - 1, 48, H), BF16),
                vmem((48, H), BF16),
                vmem((48, H), BF16),
                vmem((2 * G, 48, H), BF16),
                vmem((3, F, F), BF16),
                vmem((T, F), F32),
                dma,
                dma((Z,)),
                dma,
                dma,
                dma((2,)),
                dma((3,)),
                dma((5,)),
                dma,
                dma,
                dma,
                dma,
                dma((4,)),
                dma((4,)),
                dma((2,)),
                dma((2,)),
                dma((2, 2)),
                dma((2, 2)),
                dma((2,)),
                dma((2,)),
                dma((3,)),
                dma((3,)),
                dma((2, 2)),
                dma((2, 2)),
                dma((4,)),
                dma((4,)),
            ],
            compiler_params=pltpu.CompilerParams(
                collective_id=0, has_side_effects=True, vmem_limit_bytes=54640 * 1024
            ),
        )(
            queries, keys, values, pltpu.with_memory_space_constraint(rates.reshape(1, T), pltpu.HBM),
            fast_gate.reshape(F, F), fast_up.reshape(F, F), fast_down.reshape(F, F), pltpu.with_memory_space_constraint(out_gain.reshape(1, F), pltpu.HBM),
        )

    return jax.shard_map(
        step,
        mesh=mesh,
        in_specs=(
            P(("ctx", "head"), None),
            P(("ctx", "head"), None),
            P(("ctx", "head"), None),
            P("ctx", "head"),
            P("head", None, None),
            P("head", None, None),
            P("head", None, None),
            P("head"),
        ),
        out_specs=P("ctx", "head"),
        check_vma=False,
    )
```

```python
import functools
import math

import jax
import jax.numpy as jnp
from jax import lax
from jax.experimental import pallas as pl
from jax.experimental.pallas import tpu as pltpu
from jax.sharding import PartitionSpec as P

AHD = 128
TQ = 256
X = 4
EPS = 1e-06
RMS_EPS = 1e-05
NEG = -1e30
MESH = pl.DeviceIdType.MESH
NT = (((1,), (1,)), ((), ()))
TN = (((0,), (0,)), ((), ()))
NN = (((1,), (0,)), ((), ()))
F32 = jnp.float32
BF16 = jnp.bfloat16


def dot(a, b, dims):
    return lax.dot_general(a, b, dims, preferred_element_type=F32)


def sigmoid(a):
    return 1.0 / (1.0 + jnp.exp(-a))


def kernel(
    sizes,
    q_in, k_in, v_in, rates_in, gate_in, up_in, down_in, gain_in,
    out,
    stage, qbuf, kv, rate_row, gain, rates, weights, casts, hidden, target, ggate, gup,
    part, core_in, xs, x_in, y_own, y_in, far_in, hop_out, hop_in, gathered, renormed, attended,
    kv_send, kv_recv, q_send, q_recv, own_sem, in_sem, w_sem, h1_send, h1_recv, h2_send, h2_recv,
    c_send, c_recv, hop_send, hop_recv, x_send, x_recv, y_send, y_recv, g_send, g_recv, gx_send, gx_recv, gc_send, gc_recv,
):
    Y, Z, T, F, B = sizes
    C = 2 * X * Y
    H = F // 2
    G = X * Y
    HY = Y // 2
    rem = lax.rem
    c = lax.axis_index("ctx")
    z = lax.axis_index("head")
    core = rem(c, 2)
    chip = lax.div(c, 2)
    y = rem(chip, Y)
    x = lax.div(chip, Y)
    other = 1 - core
    mate = (c + 1 - 2 * core, z)
    xp, xm, xo = rem(x + 1, X), rem(x + X - 1, X), rem(x + 2, X)

    def at(xx, yy):
        return ((xx * Y + yy) * 2 + core, z)

    def remote(src, dst, send, recv, device):
        return pltpu.make_async_remote_copy(
            src_ref=src, dst_ref=dst, send_sem=send, recv_sem=recv, device_id=device, device_id_type=MESH
        )

    staging = [pltpu.make_async_copy(ref, stage.at[n], in_sem.at[n]) for n, ref in enumerate((k_in, v_in, q_in))]
    sources = ((gate_in, weights.at[0]), (up_in, weights.at[1]), (down_in, weights.at[2]), (rates_in, rate_row), (gain_in, gain))
    loading = [pltpu.make_async_copy(src, dst, w_sem.at[m]) for m, (src, dst) in enumerate(sources)]
    staging[0].start()
    staging[1].start()
    barrier = pltpu.get_barrier_semaphore()
    partners = [(c, rem(z + d, Z)) for d in range(1, Z)]
    partners += [at(xp, y), at(xm, y), at(xo, y), mate]
    partners += [at(x, rem(y + d, Y)) for d in range(1, Y)]
    partners += [(rem(c + 2, C), z), (rem(c + C - 2, C), z)]
    for partner in partners:
        pl.semaphore_signal(barrier, inc=1, device_id=partner, device_id_type=MESH)
    for copy in loading + staging[2:]:
        copy.start()
    pl.semaphore_wait(barrier, len(partners))

    def columns(t):
        return pl.ds(pl.multiple_of(t * F, F), F)

    def kv_copy(d):
        t = rem(z + d, Z)
        rows = pl.ds(2 * T + z * B, B)
        return remote(
            stage.at[pl.ds(0, 2), :, columns(t)], kv.at[:, rows, :], kv_send, kv_recv.at[d], (c, t)
        )

    def q_copy(d):
        t = rem(z + d, Z)
        return remote(
            stage.at[2, :, columns(t)], qbuf.at[pl.ds(z * B, B), :], q_send, q_recv, (c, t)
        )

    order = []
    for d in range(1, Z // 2):
        order += [d, Z - d]
    order.append(Z // 2)
    staging[0].wait()
    staging[1].wait()
    for d in order:
        kv_copy(d).start()
    own_kv = pltpu.make_async_copy(
        stage.at[pl.ds(0, 2), :, columns(z)], kv.at[:, pl.ds(2 * T + z * B, B), :], own_sem.at[0]
    )
    own_kv.start()

    @pl.when(c == 0)
    def _():
        zeros = jnp.zeros((T, F), BF16)
        kv[0, pl.ds(T, T), :] = zeros
        kv[1, pl.ds(T, T), :] = zeros

    @pl.when(c < 2)
    def _():
        zeros = jnp.zeros((T, F), BF16)
        kv[0, pl.ds(0, T), :] = zeros
        kv[1, pl.ds(0, T), :] = zeros

    for copy in loading:
        copy.wait()
    owner = core * G + x * Y + y
    group = pl.ds(pl.multiple_of(lax.div(owner * 8, 128) * 128, 128), 128)
    inside = pl.multiple_of(rem(owner * 8, 128), 8)
    for m in range(3):
        casts[m] = weights[m].astype(BF16)
        weights[m, 0:128, :] = weights[m, :, group].T
    rates[...] = jnp.broadcast_to(rate_row[...], (128, T)).T

    def all_of(ref, send, recv):
        return remote(ref, ref, send, recv, mate)

    def ahead(s):
        return remote(
            kv.at[:, pl.ds(2 * T + s * B, B), :],
            kv.at[:, pl.ds(s * B, B), :],
            h2_send,
            h2_recv,
            (rem(c + 2, C), z),
        )

    all_ahead = all_of(kv.at[:, pl.ds(0, T), :], h2_send, h2_recv)
    across = remote(
        kv.at[:, pl.ds((1 - core) * 2 * T, T), :], kv.at[:, pl.ds(T, T), :], h1_send, h1_recv, mate
    )

    def turn(i):
        return jnp.where(rem(i, 2) == 1, lax.div(i + 1, 2), rem(Z - lax.div(i, 2), Z))

    def update(i, carry):
        d = turn(i)
        s = rem(z + Z - d, Z)

        @pl.when(i == 0)
        def _():
            own_kv.wait()

        @pl.when(i > 0)
        def _():
            kv_copy(d).wait_recv()

        @pl.when(c + 2 < C)
        def _():
            ahead(s).start()

        rows = pl.ds(pl.multiple_of(s * B, B), B)
        here = pl.ds(pl.multiple_of(2 * T + s * B, B), B)
        k = kv[0, here, :]
        rate = jnp.concatenate([rates[rows, :]] * (F // 128), axis=1)
        aim = (rate * kv[1, here, :].astype(F32)).astype(BF16)
        target[rows, :] = aim
        pre_gate = dot(k, casts[0], NN)
        pre_up = dot(k, casts[1], NN)
        back = dot(aim, casts[2], NT)
        sig = sigmoid(pre_gate)
        sil = pre_gate * sig
        hidden[rows, :] = (sil * pre_up).astype(BF16)
        ggate[rows, :] = (back * pre_up * (sig * (1.0 + pre_gate * (1.0 - sig)))).astype(BF16)
        gup[rows, :] = (back * sil).astype(BF16)
        return carry

    lax.fori_loop(0, Z, update, 0)

    staging[2].wait()
    for d in order:
        q_copy(d).start()
    own_q = pltpu.make_async_copy(stage.at[2, :, columns(z)], qbuf.at[pl.ds(z * B, B), :], own_sem.at[1])
    own_q.start()

    here = pl.ds(2 * T, T)

    def packed(step):
        low = step[:, :H].reshape(G, 8, H)
        high = step[:, H:].reshape(G, 8, H)
        return jnp.concatenate([low, high], axis=1).astype(BF16)

    def steps(half):
        cols = pl.ds(pl.multiple_of(half * H, H), H)
        rows = pl.ds(half * G, G)
        part[rows, 0:16, :] = packed(dot(ggate[:, cols], kv[0, here, :], TN))
        part[rows, 16:32, :] = packed(dot(gup[:, cols], kv[0, here, :], TN))
        part[rows, 32:48, :] = packed(dot(target[:, cols], hidden[...], TN))

    blocks = (xp, xm, xo, x)

    def core_copy(j):
        return remote(
            part.at[pl.ds(other * G + blocks[j] * Y, Y)],
            core_in.at[pl.ds(blocks[j] * Y, Y)],
            c_send.at[j],
            c_recv.at[j],
            mate,
        )

    steps(other)
    for j in range(4):
        core_copy(j).start()
    steps(core)

    def chip_sum(j):
        core_copy(j).wait_recv()
        return part[pl.ds(core * G + blocks[j] * Y, Y)].astype(F32) + core_in[pl.ds(blocks[j] * Y, Y)].astype(F32)

    def half_of(xx, side):
        return pl.ds(xx * Y + side * HY, HY)

    def x_copy(j, side):
        return remote(
            xs.at[half_of(blocks[j], side)],
            x_in.at[j, pl.ds(side * HY, HY)],
            x_send.at[j, side],
            x_recv.at[j, side],
            at(blocks[j], y),
        )

    def y_copy(which, t):
        into = (y_in, far_in)[which]
        return remote(
            xs.at[(x, xo)[which] * Y + t],
            into.at[rem(t - y + Y, Y) - 1],
            y_send.at[which],
            y_recv.at[which],
            at(x, t),
        )

    hop = remote(hop_out, hop_in, hop_send.at[0], hop_recv.at[0], at(xo, y))
    all_y = all_of(y_in, y_send.at[0], y_recv.at[0])
    all_far = all_of(far_in, y_send.at[1], y_recv.at[1])
    near = lax.div(y, HY)
    sides = (1 - near, near)
    others = [(1 - near) * HY + e for e in range(HY)]
    close = [near * HY + rem(y + e, HY) for e in range(1, HY)]

    for j in range(2):
        xs[pl.ds(blocks[j] * Y, Y)] = chip_sum(j).astype(BF16)
        x_copy(j, sides[0]).start()
    for j in range(2):
        x_copy(j, sides[1]).start()
    y_own[...] = chip_sum(2)
    far = y_own[y]
    xs[pl.ds(xo * Y, Y)] = y_own[...].astype(BF16)
    for t in others + close:
        y_copy(1, t).start()
    y_own[...] = chip_sum(3)

    @pl.when(core == 0)
    def _():
        across.start()

    for side, peers in zip(sides, (others, close)):
        rows = pl.ds(side * HY, HY)
        for j in range(2):
            x_copy(j, side).wait_recv()
        y_own[rows] = y_own[rows] + x_in[0, rows].astype(F32) + x_in[1, rows].astype(F32)
        xs[half_of(x, side)] = y_own[rows].astype(BF16)
        for t in peers:
            y_copy(0, t).start()
    all_far.wait_recv()
    for d in range(1, Y):
        far = far + far_in[d - 1].astype(F32)
    hop_out[...] = far.astype(BF16)
    hop.start()

    @pl.when(c >= 2)
    def _():
        all_ahead.wait_recv()

    @pl.when((core == 1) & (c >= 2))
    def _():
        across.start()

    all_y.wait_recv()
    total = y_own[y]
    for d in range(1, Y):
        total = total + y_in[d - 1].astype(F32)
    hop.wait_recv()
    hop.wait_send()
    total = total + hop_in[...].astype(F32)
    for m in range(3):
        before = weights[m, pl.ds(inside, 8), :]
        norm_before = jnp.sqrt(jnp.sum(before * before, axis=1, keepdims=True) + EPS)
        low = before[:, :H] + total[m * 16 : m * 16 + 8]
        high = before[:, H:] + total[m * 16 + 8 : m * 16 + 16]
        squares = jnp.sum(low * low, axis=1, keepdims=True) + jnp.sum(high * high, axis=1, keepdims=True)
        ratio = norm_before / jnp.sqrt(squares + EPS)
        gathered[owner, m * 16 : m * 16 + 16, :] = jnp.concatenate([low * ratio, high * ratio], axis=0).astype(BF16)

    def gy_copy(which, t, sem):
        block = gathered.at[core * G + (x, xo)[which] * Y + y]
        return remote(block, block, g_send.at[sem], g_recv.at[sem], at(x, t))

    def gx_copy(j, side):
        group = gathered.at[pl.ds(core * G + x * Y + side * HY, HY)]
        return remote(group, group, gx_send.at[j, side], gx_recv.at[j, side], at(blocks[j], y))

    def gc_copy(j, side):
        group = gathered.at[pl.ds(core * G + blocks[j] * Y + side * HY, HY)]
        return remote(group, group, gc_send.at[j, side], gc_recv.at[j, side], mate)

    opposite = remote(gathered.at[owner], gathered.at[owner], hop_send.at[1], hop_recv.at[1], at(xo, y))
    all_gy = [
        all_of(gathered.at[pl.ds(0, n)], g_send.at[sem], g_recv.at[sem]) for sem, n in enumerate((HY - 1, HY, Y - 1))
    ]
    opposite.start()
    for t in close:
        gy_copy(0, t, 0).start()
    for t in others:
        gy_copy(0, t, 1).start()

    all_q = all_of(qbuf.at[pl.ds(0, (Z - 1) * B), :], q_send, q_recv)
    all_q.wait_recv()
    own_q.wait()

    @pl.when((core == 1) | (c >= 2))
    def _():
        across.wait_recv()

    tiles = T // TQ
    units = (F // AHD) * tiles
    span = 2 * T + TQ
    r_at = lax.broadcasted_iota(jnp.int32, (TQ, TQ), 0)
    c_at = lax.broadcasted_iota(jnp.int32, (TQ, TQ), 1)
    after = c_at > r_at
    k_at = lax.broadcasted_iota(jnp.int32, (1, span), 1)
    factor = math.log2(math.e) / math.sqrt(AHD)

    def attend(u, carry):
        head = lax.div(u, tiles)
        start = pl.multiple_of(rem(u, tiles) * TQ, TQ)
        lanes = pl.ds(pl.multiple_of(head * AHD, AHD), AHD)
        keys = pl.ds(start, span)
        rows = pl.ds(start, TQ)
        scores = dot(qbuf[rows, lanes], kv[0, keys, lanes], NT)
        bias = jnp.where(k_at + start >= 2 * T - c * T, 0.0, NEG)
        scores = scores + bias
        first = jnp.where(after, scores[:, :TQ], NEG)
        last = jnp.where(after, NEG, scores[:, 2 * T :])
        scores = jnp.concatenate([first, scores[:, TQ : 2 * T], last], axis=1)
        peak = jnp.max(scores, axis=1, keepdims=True)
        expo = jnp.exp2((scores - peak) * factor)
        total = jnp.sum(expo, axis=1, keepdims=True)
        mixed = dot(expo.astype(BF16), kv[1, keys, lanes], NN)
        attended[rows, lanes] = mixed / total
        return carry

    cuts = [units * n // 16 for n in (0, 6, 8, 10, 16)]
    lax.fori_loop(cuts[0], cuts[1], attend, 0)
    opposite.wait_recv()
    for t in others + close:
        gy_copy(1, t, 2).start()
    lax.fori_loop(cuts[1], cuts[2], attend, 0)
    all_gy[0].wait_recv()
    for j in range(2):
        gx_copy(j, near).start()
    lax.fori_loop(cuts[2], cuts[3], attend, 0)
    all_gy[1].wait_recv()
    for j in range(2):
        gx_copy(j, 1 - near).start()
    for side in sides:
        gc_copy(3, side).start()
    lax.fori_loop(cuts[3], cuts[4], attend, 0)

    all_of(kv.at[:, pl.ds(0, (Z - 1) * B), :], kv_send, h1_recv).wait_send()
    all_q.wait_send()

    @pl.when(c + 2 < C)
    def _():
        all_ahead.wait_send()

    @pl.when((core == 0) | (c >= 2))
    def _():
        across.wait_send()

    for j in range(4):
        core_copy(j).wait_send()
    for j in range(2):
        for side in range(2):
            x_copy(j, side).wait_send()
    all_y.wait_send()
    all_far.wait_send()
    opposite.wait_send()
    all_gy[0].wait_send()
    all_gy[1].wait_send()

    for side in (near, 1 - near):
        for j in range(2):
            gx_copy(j, side).wait_recv()
            gc_copy(1 - j, side).start()
    all_gy[2].wait_recv()
    for side in sides:
        gc_copy(2, side).start()

    def unpack(half):
        rows = pl.ds(pl.multiple_of(half * H, H), H)
        for m in range(3):
            block = gathered[pl.ds(half * G, G), m * 16 : m * 16 + 16, :].astype(F32)
            renormed[m, rows, :H] = block[:, :8].reshape(H, H).astype(BF16)
            renormed[m, rows, H:] = block[:, 8:].reshape(H, H).astype(BF16)

    def inner(half):
        cols = pl.ds(pl.multiple_of(half * H, H), H)
        gate = dot(qbuf[...], renormed[0, cols, :], NT)
        up = dot(qbuf[...], renormed[1, cols, :], NT)
        hidden[:, cols] = (gate * sigmoid(gate) * up).astype(BF16)

    unpack(core)
    inner(core)
    for j in range(4):
        for side in sides:
            gc_copy(j, side).wait_recv()
    unpack(other)
    inner(other)

    def read_rows(i, carry):
        rows = pl.ds(pl.multiple_of(i * TQ, TQ), TQ)
        read = dot(hidden[rows, :], renormed[2], NT)
        scale = lax.rsqrt(jnp.mean(read * read, axis=1, keepdims=True) + RMS_EPS)
        out[rows, :] = (attended[rows, :] + read * scale * gain[...]).astype(BF16)
        return carry

    lax.fori_loop(0, T // TQ, read_rows, 0)

    all_gy[2].wait_send()
    for j in range(2):
        for side in range(2):
            gx_copy(j, side).wait_send()
    for j in range(4):
        for side in sides:
            gc_copy(j, side).wait_send()


def solution(mesh):
    C, Z = mesh.shape["ctx"], mesh.shape["head"]
    Y = C // (2 * X)

    def step(queries, keys, values, rates, fast_gate, fast_up, fast_down, out_gain):
        B = queries.shape[0]
        T, F = rates.shape[0], fast_gate.shape[-1]
        H, G = F // 2, X * Y
        dma = pltpu.SemaphoreType.DMA
        vmem = pltpu.VMEM
        any_space = pl.BlockSpec(memory_space=pltpu.HBM)
        in_vmem = pl.BlockSpec(memory_space=pltpu.VMEM)
        return pl.pallas_call(
            functools.partial(kernel, (Y, Z, T, F, B)),
            out_shape=jax.ShapeDtypeStruct((T, F), BF16),
            in_specs=[any_space] * 8,
            out_specs=in_vmem,
            scratch_shapes=[
                vmem((3, B, Z * F), BF16),
                vmem((T, F), BF16),
                vmem((2, 3 * T, F), BF16),
                vmem((1, T), F32),
                vmem((1, F), F32),
                vmem((T, 128), F32),
                vmem((3, F, F), F32),
                vmem((3, F, F), BF16),
                vmem((T, F), BF16),
                vmem((T, F), BF16),
                vmem((T, F), BF16),
                vmem((T, F), BF16),
                vmem((2 * G, 48, H), BF16),
                vmem((G, 48, H), BF16),
                vmem((G, 48, H), BF16),
                vmem((2, Y, 48, H), BF16),
                vmem((Y, 48, H), F32),
                vmem((Y - 1, 48, H), BF16),
                vmem((Y - 1, 48, H), BF16),
                vmem((48, H), BF16),
                vmem((48, H), BF16),
                vmem((2 * G, 48, H), BF16),
                vmem((3, F, F), BF16),
                vmem((T, F), F32),
                dma,
                dma((Z,)),
                dma,
                dma,
                dma((2,)),
                dma((3,)),
                dma((5,)),
                dma,
                dma,
                dma,
                dma,
                dma((4,)),
                dma((4,)),
                dma((2,)),
                dma((2,)),
                dma((2, 2)),
                dma((2, 2)),
                dma((2,)),
                dma((2,)),
                dma((3,)),
                dma((3,)),
                dma((2, 2)),
                dma((2, 2)),
                dma((4, 2)),
                dma((4, 2)),
            ],
            compiler_params=pltpu.CompilerParams(
                collective_id=0, has_side_effects=True, vmem_limit_bytes=54640 * 1024
            ),
        )(
            queries, keys, values, pltpu.with_memory_space_constraint(rates.reshape(1, T), pltpu.HBM),
            fast_gate.reshape(F, F), fast_up.reshape(F, F), fast_down.reshape(F, F), pltpu.with_memory_space_constraint(out_gain.reshape(1, F), pltpu.HBM),
        )

    return jax.shard_map(
        step,
        mesh=mesh,
        in_specs=(
            P(("ctx", "head"), None),
            P(("ctx", "head"), None),
            P(("ctx", "head"), None),
            P("ctx", "head"),
            P("head", None, None),
            P("head", None, None),
            P("head", None, None),
            P("head"),
        ),
        out_specs=P("ctx", "head"),
        check_vma=False,
    )
```

```python
import functools
import math

import jax
import jax.numpy as jnp
from jax import lax
from jax.experimental import pallas as pl
from jax.experimental.pallas import tpu as pltpu
from jax.sharding import PartitionSpec as P

AHD = 128
TQ = 256
X = 4
EPS = 1e-06
RMS_EPS = 1e-05
NEG = -1e30
MESH = pl.DeviceIdType.MESH
NT = (((1,), (1,)), ((), ()))
TN = (((0,), (0,)), ((), ()))
NN = (((1,), (0,)), ((), ()))
F32 = jnp.float32
BF16 = jnp.bfloat16


def dot(a, b, dims):
    return lax.dot_general(a, b, dims, preferred_element_type=F32)


def sigmoid(a):
    return 1.0 / (1.0 + jnp.exp(-a))


def kernel(
    sizes,
    q_in, k_in, v_in, rates_in, gate_in, up_in, down_in, gain_in,
    out,
    stage, qbuf, kv, rate_row, gain, rates, weights, casts, hidden, target, ggate, gup,
    part, core_in, xs, x_in, y_own, y_in, far_in, hop_out, hop_in, gathered, renormed, attended,
    kv_send, kv_recv, q_send, q_recv, own_sem, in_sem, w_sem, h1_send, h1_recv, h2_send, h2_recv,
    c_send, c_recv, hop_send, hop_recv, x_send, x_recv, y_send, y_recv, g_send, g_recv, gx_send, gx_recv, gc_send, gc_recv,
):
    Y, Z, T, F, B = sizes
    C = 2 * X * Y
    H = F // 2
    G = X * Y
    HY = Y // 2
    rem = lax.rem
    c = lax.axis_index("ctx")
    z = lax.axis_index("head")
    core = rem(c, 2)
    chip = lax.div(c, 2)
    y = rem(chip, Y)
    x = lax.div(chip, Y)
    other = 1 - core
    mate = (c + 1 - 2 * core, z)
    xp, xm, xo = rem(x + 1, X), rem(x + X - 1, X), rem(x + 2, X)

    def at(xx, yy):
        return ((xx * Y + yy) * 2 + core, z)

    def remote(src, dst, send, recv, device):
        return pltpu.make_async_remote_copy(
            src_ref=src, dst_ref=dst, send_sem=send, recv_sem=recv, device_id=device, device_id_type=MESH
        )

    staging = [pltpu.make_async_copy(ref, stage.at[n], in_sem.at[n]) for n, ref in enumerate((k_in, v_in, q_in))]
    sources = ((gate_in, weights.at[0]), (up_in, weights.at[1]), (down_in, weights.at[2]), (rates_in, rate_row), (gain_in, gain))
    loading = [pltpu.make_async_copy(src, dst, w_sem.at[m]) for m, (src, dst) in enumerate(sources)]
    staging[0].start()
    staging[1].start()
    barrier = pltpu.get_barrier_semaphore()
    partners = [(c, rem(z + d, Z)) for d in range(1, Z)]
    partners += [at(xp, y), at(xm, y), at(xo, y), mate]
    partners += [at(x, rem(y + d, Y)) for d in range(1, Y)]
    partners += [(rem(c + 2, C), z), (rem(c + C - 2, C), z)]
    for partner in partners:
        pl.semaphore_signal(barrier, inc=1, device_id=partner, device_id_type=MESH)
    for copy in loading + staging[2:]:
        copy.start()
    pl.semaphore_wait(barrier, len(partners))

    def columns(t):
        return pl.ds(pl.multiple_of(t * F, F), F)

    def kv_copy(d):
        t = rem(z + d, Z)
        rows = pl.ds(2 * T + z * B, B)
        return remote(
            stage.at[pl.ds(0, 2), :, columns(t)], kv.at[:, rows, :], kv_send, kv_recv.at[d], (c, t)
        )

    def q_copy(d):
        t = rem(z + d, Z)
        return remote(
            stage.at[2, :, columns(t)], qbuf.at[pl.ds(z * B, B), :], q_send, q_recv, (c, t)
        )

    order = []
    for d in range(1, Z // 2):
        order += [d, Z - d]
    order.append(Z // 2)
    staging[0].wait()
    staging[1].wait()
    for d in order:
        kv_copy(d).start()
    own_kv = pltpu.make_async_copy(
        stage.at[pl.ds(0, 2), :, columns(z)], kv.at[:, pl.ds(2 * T + z * B, B), :], own_sem.at[0]
    )
    own_kv.start()

    @pl.when(c == 0)
    def _():
        zeros = jnp.zeros((T, F), BF16)
        kv[0, pl.ds(T, T), :] = zeros
        kv[1, pl.ds(T, T), :] = zeros

    @pl.when(c < 2)
    def _():
        zeros = jnp.zeros((T, F), BF16)
        kv[0, pl.ds(0, T), :] = zeros
        kv[1, pl.ds(0, T), :] = zeros

    for copy in loading:
        copy.wait()
    owner = core * G + x * Y + y
    group = pl.ds(pl.multiple_of(lax.div(owner * 8, 128) * 128, 128), 128)
    inside = pl.multiple_of(rem(owner * 8, 128), 8)
    for m in range(3):
        casts[m] = weights[m].astype(BF16)
        weights[m, 0:128, :] = weights[m, :, group].T
    rates[...] = jnp.broadcast_to(rate_row[...], (128, T)).T

    def all_of(ref, send, recv):
        return remote(ref, ref, send, recv, mate)

    def ahead(s):
        return remote(
            kv.at[:, pl.ds(2 * T + s * B, B), :],
            kv.at[:, pl.ds(s * B, B), :],
            h2_send,
            h2_recv,
            (rem(c + 2, C), z),
        )

    all_ahead = all_of(kv.at[:, pl.ds(0, T), :], h2_send, h2_recv)
    across = remote(
        kv.at[:, pl.ds((1 - core) * 2 * T, T), :], kv.at[:, pl.ds(T, T), :], h1_send, h1_recv, mate
    )

    def turn(i):
        return jnp.where(rem(i, 2) == 1, lax.div(i + 1, 2), rem(Z - lax.div(i, 2), Z))

    def update(i, carry):
        d = turn(i)
        s = rem(z + Z - d, Z)

        @pl.when(i == 0)
        def _():
            own_kv.wait()

        @pl.when(i > 0)
        def _():
            kv_copy(d).wait_recv()

        @pl.when(c + 2 < C)
        def _():
            ahead(s).start()

        rows = pl.ds(pl.multiple_of(s * B, B), B)
        here = pl.ds(pl.multiple_of(2 * T + s * B, B), B)
        k = kv[0, here, :]
        rate = jnp.concatenate([rates[rows, :]] * (F // 128), axis=1)
        aim = (rate * kv[1, here, :].astype(F32)).astype(BF16)
        target[rows, :] = aim
        pre_gate = dot(k, casts[0], NN)
        pre_up = dot(k, casts[1], NN)
        back = dot(aim, casts[2], NT)
        sig = sigmoid(pre_gate)
        sil = pre_gate * sig
        hidden[rows, :] = (sil * pre_up).astype(BF16)
        ggate[rows, :] = (back * pre_up * (sig * (1.0 + pre_gate * (1.0 - sig)))).astype(BF16)
        gup[rows, :] = (back * sil).astype(BF16)
        return carry

    lax.fori_loop(0, Z, update, 0)

    staging[2].wait()
    for d in order:
        q_copy(d).start()
    own_q = pltpu.make_async_copy(stage.at[2, :, columns(z)], qbuf.at[pl.ds(z * B, B), :], own_sem.at[1])
    own_q.start()

    here = pl.ds(2 * T, T)

    def packed(step):
        low = step[:, :H].reshape(G, 8, H)
        high = step[:, H:].reshape(G, 8, H)
        return jnp.concatenate([low, high], axis=1).astype(BF16)

    def steps(half):
        cols = pl.ds(pl.multiple_of(half * H, H), H)
        rows = pl.ds(half * G, G)
        part[rows, 0:16, :] = packed(dot(ggate[:, cols], kv[0, here, :], TN))
        part[rows, 16:32, :] = packed(dot(gup[:, cols], kv[0, here, :], TN))
        part[rows, 32:48, :] = packed(dot(target[:, cols], hidden[...], TN))

    blocks = (xp, xm, xo, x)

    def core_copy(j):
        return remote(
            part.at[pl.ds(other * G + blocks[j] * Y, Y)],
            core_in.at[pl.ds(blocks[j] * Y, Y)],
            c_send.at[j],
            c_recv.at[j],
            mate,
        )

    steps(other)
    for j in range(4):
        core_copy(j).start()
    steps(core)

    def chip_sum(j):
        core_copy(j).wait_recv()
        return part[pl.ds(core * G + blocks[j] * Y, Y)].astype(F32) + core_in[pl.ds(blocks[j] * Y, Y)].astype(F32)

    def half_of(xx, side):
        return pl.ds(xx * Y + side * HY, HY)

    def x_copy(j, side):
        return remote(
            xs.at[half_of(blocks[j], side)],
            x_in.at[j, pl.ds(side * HY, HY)],
            x_send.at[j, side],
            x_recv.at[j, side],
            at(blocks[j], y),
        )

    def y_copy(which, t):
        into = (y_in, far_in)[which]
        return remote(
            xs.at[(x, xo)[which] * Y + t],
            into.at[rem(t - y + Y, Y) - 1],
            y_send.at[which],
            y_recv.at[which],
            at(x, t),
        )

    hop = remote(hop_out, hop_in, hop_send.at[0], hop_recv.at[0], at(xo, y))
    all_y = all_of(y_in, y_send.at[0], y_recv.at[0])
    all_far = all_of(far_in, y_send.at[1], y_recv.at[1])
    near = lax.div(y, HY)
    sides = (1 - near, near)
    others = [(1 - near) * HY + e for e in range(HY)]
    close = [near * HY + rem(y + e, HY) for e in range(1, HY)]

    for j in range(2):
        xs[pl.ds(blocks[j] * Y, Y)] = chip_sum(j).astype(BF16)
        x_copy(j, sides[0]).start()
    for j in range(2):
        x_copy(j, sides[1]).start()
    y_own[...] = chip_sum(2)
    far = y_own[y]
    xs[pl.ds(xo * Y, Y)] = y_own[...].astype(BF16)
    for t in others + close:
        y_copy(1, t).start()
    y_own[...] = chip_sum(3)

    @pl.when(core == 0)
    def _():
        across.start()

    for side, peers in zip(sides, (others, close)):
        rows = pl.ds(side * HY, HY)
        for j in range(2):
            x_copy(j, side).wait_recv()
        y_own[rows] = y_own[rows] + x_in[0, rows].astype(F32) + x_in[1, rows].astype(F32)
        xs[half_of(x, side)] = y_own[rows].astype(BF16)
        for t in peers:
            y_copy(0, t).start()
    all_far.wait_recv()
    for d in range(1, Y):
        far = far + far_in[d - 1].astype(F32)
    hop_out[...] = far.astype(BF16)
    hop.start()

    all_y.wait_recv()
    total = y_own[y]
    for d in range(1, Y):
        total = total + y_in[d - 1].astype(F32)
    hop.wait_recv()
    hop.wait_send()
    total = total + hop_in[...].astype(F32)
    for m in range(3):
        before = weights[m, pl.ds(inside, 8), :]
        norm_before = jnp.sqrt(jnp.sum(before * before, axis=1, keepdims=True) + EPS)
        low = before[:, :H] + total[m * 16 : m * 16 + 8]
        high = before[:, H:] + total[m * 16 + 8 : m * 16 + 16]
        squares = jnp.sum(low * low, axis=1, keepdims=True) + jnp.sum(high * high, axis=1, keepdims=True)
        ratio = norm_before / jnp.sqrt(squares + EPS)
        gathered[owner, m * 16 : m * 16 + 16, :] = jnp.concatenate([low * ratio, high * ratio], axis=0).astype(BF16)

    def gy_copy(which, t, sem):
        block = gathered.at[core * G + (x, xo)[which] * Y + y]
        return remote(block, block, g_send.at[sem], g_recv.at[sem], at(x, t))

    def gx_copy(j, side):
        group = gathered.at[pl.ds(core * G + x * Y + side * HY, HY)]
        return remote(group, group, gx_send.at[j, side], gx_recv.at[j, side], at(blocks[j], y))

    def gc_copy(j, side):
        group = gathered.at[pl.ds(core * G + blocks[j] * Y + side * HY, HY)]
        return remote(group, group, gc_send.at[j, side], gc_recv.at[j, side], mate)

    opposite = remote(gathered.at[owner], gathered.at[owner], hop_send.at[1], hop_recv.at[1], at(xo, y))
    all_gy = [
        all_of(gathered.at[pl.ds(0, n)], g_send.at[sem], g_recv.at[sem]) for sem, n in enumerate((HY - 1, HY, Y - 1))
    ]
    opposite.start()
    for t in close:
        gy_copy(0, t, 0).start()
    for t in others:
        gy_copy(0, t, 1).start()

    @pl.when(c >= 2)
    def _():
        all_ahead.wait_recv()

    @pl.when((core == 1) & (c >= 2))
    def _():
        across.start()

    all_q = all_of(qbuf.at[pl.ds(0, (Z - 1) * B), :], q_send, q_recv)
    all_q.wait_recv()
    own_q.wait()

    @pl.when((core == 1) | (c >= 2))
    def _():
        across.wait_recv()

    tiles = T // TQ
    units = (F // AHD) * tiles
    span = 2 * T + TQ
    r_at = lax.broadcasted_iota(jnp.int32, (TQ, TQ), 0)
    c_at = lax.broadcasted_iota(jnp.int32, (TQ, TQ), 1)
    after = c_at > r_at
    k_at = lax.broadcasted_iota(jnp.int32, (1, span), 1)
    factor = math.log2(math.e) / math.sqrt(AHD)

    def attend(u, carry):
        head = lax.div(u, tiles)
        start = pl.multiple_of(rem(u, tiles) * TQ, TQ)
        lanes = pl.ds(pl.multiple_of(head * AHD, AHD), AHD)
        keys = pl.ds(start, span)
        rows = pl.ds(start, TQ)
        scores = dot(qbuf[rows, lanes], kv[0, keys, lanes], NT)
        bias = jnp.where(k_at + start >= 2 * T - c * T, 0.0, NEG)
        scores = scores + bias
        first = jnp.where(after, scores[:, :TQ], NEG)
        last = jnp.where(after, NEG, scores[:, 2 * T :])
        scores = jnp.concatenate([first, scores[:, TQ : 2 * T], last], axis=1)
        peak = jnp.max(scores, axis=1, keepdims=True)
        expo = jnp.exp2((scores - peak) * factor)
        total = jnp.sum(expo, axis=1, keepdims=True)
        mixed = dot(expo.astype(BF16), kv[1, keys, lanes], NN)
        attended[rows, lanes] = mixed / total
        return carry

    cuts = [units * n // 16 for n in (0, 6, 8, 10, 16)]
    lax.fori_loop(cuts[0], cuts[1], attend, 0)
    opposite.wait_recv()
    for t in others + close:
        gy_copy(1, t, 2).start()
    lax.fori_loop(cuts[1], cuts[2], attend, 0)
    all_gy[0].wait_recv()
    for j in range(2):
        gx_copy(j, near).start()
    lax.fori_loop(cuts[2], cuts[3], attend, 0)
    all_gy[1].wait_recv()
    for j in range(2):
        gx_copy(j, 1 - near).start()
    for side in sides:
        gc_copy(3, side).start()
    lax.fori_loop(cuts[3], cuts[4], attend, 0)

    all_of(kv.at[:, pl.ds(0, (Z - 1) * B), :], kv_send, h1_recv).wait_send()
    all_q.wait_send()

    @pl.when(c + 2 < C)
    def _():
        all_ahead.wait_send()

    @pl.when((core == 0) | (c >= 2))
    def _():
        across.wait_send()

    for j in range(4):
        core_copy(j).wait_send()
    for j in range(2):
        for side in range(2):
            x_copy(j, side).wait_send()
    all_y.wait_send()
    all_far.wait_send()
    opposite.wait_send()
    all_gy[0].wait_send()
    all_gy[1].wait_send()

    for side in (near, 1 - near):
        for j in range(2):
            gx_copy(j, side).wait_recv()
            gc_copy(1 - j, side).start()
    all_gy[2].wait_recv()
    for side in sides:
        gc_copy(2, side).start()

    def unpack(half):
        rows = pl.ds(pl.multiple_of(half * H, H), H)
        for m in range(3):
            block = gathered[pl.ds(half * G, G), m * 16 : m * 16 + 16, :].astype(F32)
            renormed[m, rows, :H] = block[:, :8].reshape(H, H).astype(BF16)
            renormed[m, rows, H:] = block[:, 8:].reshape(H, H).astype(BF16)

    def inner(half):
        cols = pl.ds(pl.multiple_of(half * H, H), H)
        gate = dot(qbuf[...], renormed[0, cols, :], NT)
        up = dot(qbuf[...], renormed[1, cols, :], NT)
        hidden[:, cols] = (gate * sigmoid(gate) * up).astype(BF16)

    unpack(core)
    inner(core)
    for j in range(4):
        for side in sides:
            gc_copy(j, side).wait_recv()
    unpack(other)
    inner(other)

    def read_rows(i, carry):
        rows = pl.ds(pl.multiple_of(i * TQ, TQ), TQ)
        read = dot(hidden[rows, :], renormed[2], NT)
        scale = lax.rsqrt(jnp.mean(read * read, axis=1, keepdims=True) + RMS_EPS)
        out[rows, :] = (attended[rows, :] + read * scale * gain[...]).astype(BF16)
        return carry

    lax.fori_loop(0, T // TQ, read_rows, 0)

    all_gy[2].wait_send()
    for j in range(2):
        for side in range(2):
            gx_copy(j, side).wait_send()
    for j in range(4):
        for side in sides:
            gc_copy(j, side).wait_send()


def solution(mesh):
    C, Z = mesh.shape["ctx"], mesh.shape["head"]
    Y = C // (2 * X)

    def step(queries, keys, values, rates, fast_gate, fast_up, fast_down, out_gain):
        B = queries.shape[0]
        T, F = rates.shape[0], fast_gate.shape[-1]
        H, G = F // 2, X * Y
        dma = pltpu.SemaphoreType.DMA
        vmem = pltpu.VMEM
        any_space = pl.BlockSpec(memory_space=pltpu.HBM)
        in_vmem = pl.BlockSpec(memory_space=pltpu.VMEM)
        return pl.pallas_call(
            functools.partial(kernel, (Y, Z, T, F, B)),
            out_shape=jax.ShapeDtypeStruct((T, F), BF16),
            in_specs=[any_space] * 8,
            out_specs=in_vmem,
            scratch_shapes=[
                vmem((3, B, Z * F), BF16),
                vmem((T, F), BF16),
                vmem((2, 3 * T, F), BF16),
                vmem((1, T), F32),
                vmem((1, F), F32),
                vmem((T, 128), F32),
                vmem((3, F, F), F32),
                vmem((3, F, F), BF16),
                vmem((T, F), BF16),
                vmem((T, F), BF16),
                vmem((T, F), BF16),
                vmem((T, F), BF16),
                vmem((2 * G, 48, H), BF16),
                vmem((G, 48, H), BF16),
                vmem((G, 48, H), BF16),
                vmem((2, Y, 48, H), BF16),
                vmem((Y, 48, H), F32),
                vmem((Y - 1, 48, H), BF16),
                vmem((Y - 1, 48, H), BF16),
                vmem((48, H), BF16),
                vmem((48, H), BF16),
                vmem((2 * G, 48, H), BF16),
                vmem((3, F, F), BF16),
                vmem((T, F), F32),
                dma,
                dma((Z,)),
                dma,
                dma,
                dma((2,)),
                dma((3,)),
                dma((5,)),
                dma,
                dma,
                dma,
                dma,
                dma((4,)),
                dma((4,)),
                dma((2,)),
                dma((2,)),
                dma((2, 2)),
                dma((2, 2)),
                dma((2,)),
                dma((2,)),
                dma((3,)),
                dma((3,)),
                dma((2, 2)),
                dma((2, 2)),
                dma((4, 2)),
                dma((4, 2)),
            ],
            compiler_params=pltpu.CompilerParams(
                collective_id=0, has_side_effects=True, vmem_limit_bytes=54640 * 1024
            ),
        )(
            queries, keys, values, pltpu.with_memory_space_constraint(rates.reshape(1, T), pltpu.HBM),
            fast_gate.reshape(F, F), fast_up.reshape(F, F), fast_down.reshape(F, F), pltpu.with_memory_space_constraint(out_gain.reshape(1, F), pltpu.HBM),
        )

    return jax.shard_map(
        step,
        mesh=mesh,
        in_specs=(
            P(("ctx", "head"), None),
            P(("ctx", "head"), None),
            P(("ctx", "head"), None),
            P("ctx", "head"),
            P("head", None, None),
            P("head", None, None),
            P("head", None, None),
            P("head"),
        ),
        out_specs=P("ctx", "head"),
        check_vma=False,
    )
```
